32 devices in a mesh: exp: 8 (over z, x), tp: 4 (over y, core).
Axes of the slice: x: 2, y: 2, z: 4, core: 2. Of those that a mesh axis runs over, the one named last changes fastest.
Arguments:
- hidden: bfloat16 [10240, 2048], P('exp'), may hold values from -6 to 6
- cotangent: bfloat16 [10240, 2048], P(('exp', 'tp')), may hold values from -6 to 6
- norm_gains: float32 [2, 2048], replicated, may hold values from 0.5 to 1.5
- qkv_weight: bfloat16 [2048, 3, 2048], P(None, None, 'tp'), may hold values from -0.125 to 0.125
- qk_gain: float32 [2, 2048], P(None, 'tp'), may hold values from 0.5 to 1.5
- out_weight: bfloat16 [2048, 2048], P('tp'), may hold values from -0.5 to 0.5
- router_weight: bfloat16 [2048, 32], replicated, may hold values from -0.0625 to 0.0625
- gate_up: bfloat16 [64, 2048, 2, 512], P(('exp', 'tp')), may hold values from -0.125 to 0.125
- down_weight: bfloat16 [64, 512, 2048], P(('exp', 'tp')), may hold values from -4 to 4
- routes: int32 [10240, 8], P('exp'), may hold values from 0 to 31, all different within a row
- parents: int32 [8, 12], P('exp'), may hold values from 0 to 4, as said below
Outputs:
- layer_out: bfloat16 [10240, 2048], P(('exp', 'tp'))
- input_grad: bfloat16 [10240, 2048], P('exp')
- norm_gains_grad: float32 [2, 2048], replicated
- qkv_grad: float32 [2048, 3, 2048], P(None, None, 'tp')
- qk_gain_grad: float32 [2, 2048], P(None, 'tp')
- out_weight_grad: float32 [2048, 2048], P('tp')
- router_grad: float32 [2048, 32], replicated
- gate_up_grad: float32 [64, 2048, 2, 512], P(('exp', 'tp'))
- down_grad: float32 [64, 512, 2048], P(('exp', 'tp'))
The draws below stay inside these ranges and needn't reach their ends.
Inputs may be any that keep to these rules, and one draw needn't show every extreme that they name: `routes`: each row names 8 different experts. `parents`: in each row (one tree) exactly four entries are 0: those segments are branches, numbered 1 to 4 in the order of their entries; every other entry is a leaf and names its branch by that number; each branch has exactly two leaves.
All inputs are finite; a program needn't handle non-finite values.
Results may differ from the reference program's by a relative error of at most 0.025.
Values may be sent and summed in bfloat16 or wider, within the bound.
A program may use at most 448 MiB of HBM per device.

```python
import jax
import jax.numpy as jnp
from jax import lax

D = 2048
HEADS = 16
HEAD_DIM = 128
FF = 1024
TOP = 8
TRUNK = 512
BRANCH = 64
EXPERTS = 32
TREE = 1280
TOK_SLICE = 320
TOKENS = 10240
TREES_ALL = 8
CAP = 90


def draw_parents(key, part):
    key = jax.random.fold_in(key, 11)
    keys = jax.random.split(key, TREES_ALL)

    def one_tree(tree_key):
        shuffled = jax.random.permutation(tree_key, 12).astype(jnp.int32)
        return jnp.zeros((12,), jnp.int32).at[shuffled[4:]].set(1 + jnp.arange(8, dtype=jnp.int32) // 2)
    return jax.vmap(one_tree)(keys)


def levels(rng, extent, shards, smallest, high):
    loudness = 1.0
    for position, parts in shards:
        steps = jax.random.uniform(jax.random.fold_in(jax.random.fold_in(rng, 6), position), (parts,), jnp.float32, smallest / len(shards), high / len(shards))
        loudness = loudness * jnp.repeat(jnp.exp(steps), extent[position] // parts).reshape((-1,) + (1,) * (len(extent) - 1 - position))
    return loudness


def different_ones(rng, rows, number_of, top, lift):
    order = jax.random.permutation(jax.random.fold_in(rng, 1), number_of)
    boost = order
    for power in range(3):
        boost = boost * boost // number_of
    boost = boost * lift // number_of
    tickets = jax.random.randint(jax.random.fold_in(rng, 2), (rows, number_of), 0, 4096) + boost
    fixed_rows = jax.random.permutation(jax.random.fold_in(rng, 3), rows)[jnp.arange(number_of) % rows]
    tickets = jnp.where(jnp.arange(rows)[:, None] == fixed_rows[None, :], 1 << 14, tickets)
    merit = tickets * number_of + jnp.arange(number_of)
    return lax.top_k(merit.astype(jnp.int32), top)[1].astype(jnp.int32)


def bell_draw(rng, extent, deviation, limit, pieces=(), held_as=jnp.bfloat16):
    gain = levels(rng, extent, pieces, -0.22, 0.18) if pieces else 1.0
    drawn = jax.random.normal(rng, extent, jnp.float32) * deviation * gain
    return jnp.minimum(jnp.maximum(drawn, -limit), limit).astype(held_as)


def setup_inputs(seed: int = 0) -> dict:
    seeds = jax.random.split(jax.random.key(seed), 12)
    hidden = bell_draw(seeds[0], (TOKENS, D), 1.0, 6.0, ((0, 8),))
    cotangent = bell_draw(seeds[1], (TOKENS, D), 1.0, 6.0, ((0, 32),))
    norm_gains = jnp.clip(1.0 + 0.1 * jax.random.normal(seeds[2], (2, D), jnp.float32), 0.5, 1.5)
    qkv_weight = bell_draw(seeds[3], (D, 3, D), D ** -0.5, 0.125, ((2, 4),))
    qk_gain = jnp.clip(1.0 + 0.1 * jax.random.normal(seeds[4], (2, D), jnp.float32), 0.5, 1.5)
    out_weight = bell_draw(seeds[5], (D, D), (max(D // 16, 1)) ** -0.5, 0.5, ((0, 4),))
    router_weight = bell_draw(seeds[6], (D, EXPERTS), (4 * D) ** -0.5, 0.0625)
    gate_up = bell_draw(seeds[7], (2 * EXPERTS, D, 2, FF // 2), D ** -0.5, 0.125, ((0, 32),))
    down_weight = bell_draw(seeds[8], (2 * EXPERTS, FF // 2, D), (max(FF // 512, 1)) ** -0.5, 4.0, ((0, 32),))
    routes = different_ones(seeds[9], TOKENS, EXPERTS, TOP, 2048)
    parents = draw_parents(jax.random.fold_in(seeds[11], 71), 0)
    return {"hidden": hidden, "cotangent": cotangent, "norm_gains": norm_gains, "qkv_weight": qkv_weight, "qk_gain": qk_gain, "out_weight": out_weight, "router_weight": router_weight, "gate_up": gate_up, "down_weight": down_weight, "routes": routes, "parents": parents}


EPSILON = 1e-05
BASE_FREQ = 10000.0
MASKED_SCORE = -1e+30
PRECISE_MATMUL = lax.Precision.HIGHEST

@jax.custom_vjp
def low(v):
    return lax.optimization_barrier(v.astype(jnp.bfloat16)).astype(jnp.float32)

@jax.custom_vjp
def low_back(v):
    return v

def low_keep(v):
    return (low(v), None)

def low_pass(kept, grad):
    return (grad,)

def back_keep(v):
    return (v, None)

def back_low(kept, grad):
    return (low(grad),)
low.defvjp(low_keep, low_pass)
low_back.defvjp(back_keep, back_low)

def normalize(tensor):
    inverse = lax.rsqrt(lax.optimization_barrier(jnp.mean(tensor * tensor, axis=-1, keepdims=True)) + EPSILON)
    return tensor * inverse

def softmax_rows(scores):
    weights = jnp.exp(scores - lax.optimization_barrier(jnp.max(scores, axis=-1, keepdims=True)))
    return weights / lax.optimization_barrier(jnp.sum(weights, axis=-1, keepdims=True))

def tree_layout(parent_row):
    row_index = jnp.arange(TRUNK + 12 * BRANCH, dtype=jnp.int32)
    segment = jnp.where(row_index < TRUNK, 0, 1 + (row_index - TRUNK) // BRANCH).astype(jnp.int32)
    offset = jnp.where(row_index < TRUNK, row_index, (row_index - TRUNK) % BRANCH).astype(jnp.int32)
    branch = parent_row == 0
    branch_order = jnp.cumsum(branch.astype(jnp.int32)).astype(jnp.int32)
    leaf_link = (parent_row[:, None] == branch_order[None, :]) & branch[None, :] & jnp.logical_not(branch)[:, None]
    parent = jnp.zeros((13, 13), jnp.float32)
    parent = parent.at[1:, 0].set(branch.astype(jnp.float32))
    parent = parent.at[1:, 1:].set(leaf_link.astype(jnp.float32))
    ancestor = jnp.eye(13, dtype=jnp.float32) + parent + jnp.dot(parent, parent, precision=PRECISE_MATMUL)
    depth_table = jnp.concatenate([jnp.zeros((1,), jnp.int32), jnp.where(branch, 1, 2).astype(jnp.int32)])
    labels = jnp.arange(13, dtype=jnp.int32)
    member = segment[:, None] == labels[None, :]
    depth_rank = lax.optimization_barrier(jnp.sum(jnp.where(member, depth_table[None, :], 0), axis=1)).astype(jnp.int32)
    positions = offset + jnp.where(depth_rank >= 1, TRUNK, 0) + jnp.where(depth_rank == 2, BRANCH, 0)
    return (member.astype(jnp.float32), ancestor, positions.astype(jnp.int32))

def path_mask(member, ancestor, positions):
    reached_slots = jnp.dot(jnp.dot(member, ancestor, precision=PRECISE_MATMUL), member.T, precision=PRECISE_MATMUL)
    return (reached_slots > 0.5) & (positions[None, :] <= positions[:, None])

def rope_tables(positions):
    frequency = BASE_FREQ ** (-jnp.arange(0, HEAD_DIM, 2, dtype=jnp.float32) / HEAD_DIM)
    angles = positions.astype(jnp.float32)[:, None] * frequency[None, :]
    cos_half = jnp.cos(angles)
    sin_half = jnp.sin(angles)
    return (jnp.concatenate([cos_half, cos_half], axis=-1), jnp.concatenate([sin_half, sin_half], axis=-1))

def rotate(tensor, cos_table, sin_table):
    half_dim = tensor.shape[-1] // 2
    turned = jnp.concatenate([-tensor[..., half_dim:], tensor[..., :half_dim]], axis=-1)
    return tensor * cos_table[:, None, :] + turned * sin_table[:, None, :]

def slot_tables(routes, tokens):
    slice_count = tokens // TOK_SLICE
    pair_count = TOK_SLICE * TOP
    route_slices = routes.reshape(slice_count, pair_count)
    labels = jnp.arange(EXPERTS, dtype=jnp.int32)
    route_hits = (route_slices[:, :, None] == labels[None, None, :]).astype(jnp.int32)
    running = (jnp.cumsum(route_hits, axis=1) - 1).astype(jnp.int32)
    slot_index = lax.optimization_barrier(jnp.sum(route_hits * running, axis=2)).astype(jnp.int32)
    slice_ids = jnp.arange(slice_count, dtype=jnp.int32)[:, None]
    target = jnp.where(slot_index < CAP, (route_slices * slice_count + slice_ids) * CAP + slot_index, EXPERTS * slice_count * CAP).astype(jnp.int32)
    pair_ids = (slice_ids * pair_count + jnp.arange(pair_count, dtype=jnp.int32)[None, :]).astype(jnp.int32)
    slot_pairs = jnp.full((EXPERTS * slice_count * CAP,), tokens * TOP, jnp.int32)
    slot_pairs = slot_pairs.at[target.reshape(-1)].set(pair_ids.reshape(-1), mode='drop')
    slot_pairs = slot_pairs.reshape(EXPERTS, slice_count * CAP)
    return ((slot_pairs // TOP).astype(jnp.int32), slot_pairs)

def layer(hidden, norm_gains, qkv_weight, qk_gain, out_weight, router_weight, gate_up, down_weight, routes, parents):
    tokens = hidden.shape[0]
    normed_one = low(normalize(hidden) * norm_gains[0])
    qkv_all = low_back(jnp.dot(normed_one, qkv_weight.reshape(D, 3 * D), precision=PRECISE_MATMUL))
    query_all = normalize(qkv_all[:, :D]) * qk_gain[0]
    key_all = normalize(qkv_all[:, D:2 * D]) * qk_gain[1]
    value_gathered = qkv_all[:, 2 * D:]
    tree_count = tokens // TREE

    def attend(tree_block):
        query_tree, key_tree, value_tree, parent_row = tree_block
        member, ancestor, positions = tree_layout(parent_row)
        allowed = path_mask(member, ancestor, positions)
        cos_table, sin_table = rope_tables(positions)
        query_rot = low(rotate(query_tree.reshape(TREE, HEADS, HEAD_DIM), cos_table, sin_table))
        key_rot = low(rotate(key_tree.reshape(TREE, HEADS, HEAD_DIM), cos_table, sin_table))
        value_low = low(value_tree.reshape(TREE, HEADS, HEAD_DIM))
        scores = low_back(jnp.einsum('qhd,khd->hqk', query_rot, key_rot, precision=PRECISE_MATMUL) * HEAD_DIM ** (-0.5))
        attn_probs = softmax_rows(jnp.where(allowed[None], scores, MASKED_SCORE))
        context = jnp.einsum('hqk,khd->qhd', low(attn_probs), value_low, precision=PRECISE_MATMUL)
        return context.reshape(TREE, D)
    tree_shape = (tree_count, TREE, D)
    context = lax.map(jax.checkpoint(attend), (query_all.reshape(tree_shape), key_all.reshape(tree_shape), value_gathered.reshape(tree_shape), parents))
    context = low(low_back(context.reshape(tokens, D)))
    attention = low_back(jnp.dot(context, out_weight, precision=PRECISE_MATMUL))
    mixed = hidden + attention
    normed_two = low(normalize(mixed) * norm_gains[1])
    logits = low_back(jnp.dot(normed_two, router_weight, precision=PRECISE_MATMUL))
    route_probs = softmax_rows(logits)
    gate_values = jnp.take_along_axis(route_probs, routes, axis=1)
    slot_rows, slot_pairs = slot_tables(routes, tokens)
    gate_slots = jnp.concatenate([gate_values.reshape(-1), jnp.zeros((1,), jnp.float32)])[slot_pairs]
    padded_rows = jnp.concatenate([normed_two, jnp.zeros((1, D), jnp.float32)], axis=0)

    def expert(expert_block):
        rows_of, weight_in, output_weight = expert_block
        taken = padded_rows[rows_of]
        copies = low_back(jnp.broadcast_to(taken[None], (2,) + taken.shape))
        pre_act = low_back(jnp.einsum('trd,tdgf->trgf', copies, weight_in, precision=PRECISE_MATMUL))
        hidden_activation = low(jax.nn.silu(pre_act[:, :, 0]) * pre_act[:, :, 1])
        partial_output = jnp.einsum('nqo,nob->nqb', hidden_activation, output_weight, precision=PRECISE_MATMUL)
        return low_back(lax.optimization_barrier(jnp.sum(low(partial_output), axis=0)))
    halves_in = gate_up.reshape(EXPERTS, 2, D, 2, FF // 2)
    halves_out = down_weight.reshape(EXPERTS, 2, FF // 2, D)
    outputs = lax.map(jax.checkpoint(expert), (slot_rows, halves_in, halves_out))
    weighted = (gate_slots[..., None] * outputs).reshape(-1, D)
    expert_sum = jax.ops.segment_sum(weighted, slot_rows.reshape(-1), num_segments=tokens + 1)
    return mixed + expert_sum[:tokens]

def reference(hidden, cotangent, norm_gains, qkv_weight, qk_gain, out_weight, router_weight, gate_up, down_weight, routes, parents):
    primal_inputs = (hidden.astype(jnp.float32), norm_gains.astype(jnp.float32), qkv_weight.astype(jnp.float32), qk_gain.astype(jnp.float32), out_weight.astype(jnp.float32), router_weight.astype(jnp.float32), gate_up.astype(jnp.float32), down_weight.astype(jnp.float32))

    def forward(hidden_f, gains_f, qkv_f, qk_f, out_f, router_f, gate_up_f, down_f):
        return layer(hidden_f, gains_f, qkv_f, qk_f, out_f, router_f, gate_up_f, down_f, routes, parents)
    result, pullback = jax.vjp(forward, primal_inputs[0], primal_inputs[1], primal_inputs[2], primal_inputs[3], primal_inputs[4], primal_inputs[5], primal_inputs[6], primal_inputs[7])
    gradients = pullback(cotangent.astype(jnp.float32))
    return (result.astype(jnp.bfloat16), gradients[0].astype(jnp.bfloat16), gradients[1], gradients[2], gradients[3], gradients[4], gradients[5], gradients[6], gradients[7])
```

```python
import jax
import jax.numpy as jnp
from jax import lax
from jax.sharding import PartitionSpec as P

HEAD_DIM = 128
TRUNK = 512
BRANCH = 64


EPSILON = 1e-05
BASE_FREQ = 10000.0
MASKED_SCORE = -1e30
PRECISE_MATMUL = lax.Precision.HIGHEST


def normalize(tensor):
    inverse = lax.rsqrt(jnp.mean(tensor * tensor, axis=-1, keepdims=True) + EPSILON)
    return (tensor * inverse, inverse)


def norm_back(grad_in, unit, inverse, gain):
    scaled = grad_in * gain
    return inverse * (scaled - unit * jnp.mean(scaled * unit, axis=-1, keepdims=True))


def softmax_rows(scores):
    weights = jnp.exp(scores - jnp.max(scores, axis=-1, keepdims=True))
    return weights / jnp.sum(weights, axis=-1, keepdims=True)


def tree_layout(parent_row):
    row_index = jnp.arange(TRUNK + 12 * BRANCH, dtype=jnp.int32)
    segment = jnp.where(row_index < TRUNK, 0, 1 + (row_index - TRUNK) // BRANCH)
    offset = jnp.where(row_index < TRUNK, row_index, (row_index - TRUNK) % BRANCH)
    branch = parent_row == 0
    branch_order = jnp.cumsum(branch.astype(jnp.int32))
    leaf_link = (
        (parent_row[:, None] == branch_order[None, :])
        & branch[None, :]
        & jnp.logical_not(branch)[:, None]
    )
    parent = jnp.zeros((13, 13), jnp.float32)
    parent = parent.at[1:, 0].set(branch.astype(jnp.float32))
    parent = parent.at[1:, 1:].set(leaf_link.astype(jnp.float32))
    ancestor = (
        jnp.eye(13, dtype=jnp.float32) + parent + jnp.dot(parent, parent, precision=PRECISE_MATMUL)
    )
    depth_table = jnp.concatenate(
        [jnp.zeros((1,), jnp.int32), jnp.where(branch, 1, 2).astype(jnp.int32)]
    )
    labels = jnp.arange(13, dtype=jnp.int32)
    member = segment[:, None] == labels[None, :]
    depth_rank = jnp.sum(jnp.where(member, depth_table[None, :], 0), axis=1)
    positions = (
        offset + jnp.where(depth_rank >= 1, TRUNK, 0) + jnp.where(depth_rank == 2, BRANCH, 0)
    )
    return (member.astype(jnp.float32), ancestor, positions)


def path_mask(member, ancestor, positions):
    reached_slots = jnp.dot(
        jnp.dot(member, ancestor, precision=PRECISE_MATMUL), member.T, precision=PRECISE_MATMUL
    )
    return (reached_slots > 0.5) & (positions[None, :] <= positions[:, None])


def rope_tables(positions):
    frequency = BASE_FREQ ** (-jnp.arange(0, HEAD_DIM, 2, dtype=jnp.float32) / HEAD_DIM)
    angles = positions.astype(jnp.float32)[:, None] * frequency[None, :]
    cos_half = jnp.cos(angles)
    sin_half = jnp.sin(angles)
    return (
        jnp.concatenate([cos_half, cos_half], axis=-1),
        jnp.concatenate([sin_half, sin_half], axis=-1),
    )


def rotate(tensor, cos_table, sin_table):
    half_dim = tensor.shape[-1] // 2
    turned = jnp.concatenate([-tensor[..., half_dim:], tensor[..., :half_dim]], axis=-1)
    return tensor * cos_table[:, None, :] + turned * sin_table[:, None, :]


def unrotate(tensor, cos_table, sin_table):
    half_dim = tensor.shape[-1] // 2
    shifted = tensor * sin_table[:, None, :]
    return tensor * cos_table[:, None, :] + jnp.concatenate(
        [shifted[..., half_dim:], -shifted[..., :half_dim]], axis=-1
    )


def scores_of(query_tree, key_tree, member, ancestor, positions):
    allowed = path_mask(member, ancestor, positions)
    raw = jnp.einsum(
        "qhd,khd->hqk", query_tree, key_tree, preferred_element_type=jnp.float32
    ) * HEAD_DIM ** (-0.5)
    return jnp.where(allowed[None], raw, MASKED_SCORE)


def attend(tree_block):
    query_tree, key_tree, value_tree, member, ancestor, positions = tree_block
    scores = scores_of(query_tree, key_tree, member, ancestor, positions)
    top_score = jnp.max(scores, axis=2, keepdims=True)
    weights = jnp.exp(scores - top_score)
    total = jnp.sum(weights, axis=2, keepdims=True)
    attn_probs = weights / total
    context = jnp.einsum(
        "hqk,khd->qhd",
        attn_probs.astype(jnp.bfloat16),
        value_tree,
        preferred_element_type=jnp.float32,
    )
    return (context.astype(jnp.bfloat16), top_score[..., 0] + jnp.log(total[..., 0]))


def attend_back(tree_block):
    query_tree, key_tree, value_tree, context_grad, log_total, member, ancestor, positions = (
        tree_block
    )
    scores = scores_of(query_tree, key_tree, member, ancestor, positions)
    attn_probs = jnp.exp(scores - log_total[..., None])
    prob_grad = jnp.einsum(
        "qhd,khd->hqk", context_grad, value_tree, preferred_element_type=jnp.float32
    )
    score_grad = attn_probs * (prob_grad - jnp.sum(attn_probs * prob_grad, axis=2, keepdims=True))
    score_low = score_grad.astype(jnp.bfloat16)
    scale = HEAD_DIM ** (-0.5)
    query_grad = (
        jnp.einsum("hqk,khd->qhd", score_low, key_tree, preferred_element_type=jnp.float32) * scale
    )
    key_grad = (
        jnp.einsum("hqk,qhd->khd", score_low, query_tree, preferred_element_type=jnp.float32)
        * scale
    )
    value_grad = jnp.einsum(
        "hqk,qhd->khd",
        attn_probs.astype(jnp.bfloat16),
        context_grad,
        preferred_element_type=jnp.float32,
    )
    return (query_grad, key_grad, value_grad)


def shards(
    hidden,
    cotangent,
    norm_gains,
    qkv_weight,
    qk_gain,
    out_weight,
    router_weight,
    gate_up,
    down_weight,
    routes,
    parents,
):
    tp_count = lax.axis_size("tp")
    exp_count = lax.axis_size("exp")
    tp_rank = lax.axis_index("tp")
    exp_rank = lax.axis_index("exp")
    world = ("exp", "tp")
    device_count = exp_count * tp_count
    device_rank = exp_rank * tp_count + tp_rank
    rows_all, model_width = hidden.shape
    rows_own = cotangent.shape[0]
    local_width = qkv_weight.shape[2]
    local_heads = local_width // HEAD_DIM
    expert_count = router_weight.shape[1]
    half_count = gate_up.shape[0]
    ff_half = gate_up.shape[3]
    top_count = routes.shape[1]
    capacity = (9 * rows_own * top_count + 8 * expert_count - 1) // (8 * expert_count)
    cap_pad = -(-capacity // 16) * 16
    tree_count = parents.shape[0]
    tree_len = rows_all // tree_count
    own_start = tp_rank * rows_own

    own_routes = lax.dynamic_slice_in_dim(routes, own_start, rows_own, 0)
    labels = jnp.arange(expert_count, dtype=jnp.int32)
    hits = jnp.any(own_routes[:, :, None] == labels[None, None, :], axis=1)
    row_ids = jnp.arange(rows_own, dtype=jnp.int32)
    earlier = (row_ids[:, None] > row_ids[None, :]).astype(jnp.bfloat16)
    slots = jnp.dot(earlier, hits.astype(jnp.bfloat16), preferred_element_type=jnp.float32).astype(
        jnp.int32
    )
    kept = hits & (slots < capacity)
    codes = jnp.where(kept, slots, -1)
    slot_ids = jnp.arange(cap_pad, dtype=jnp.int32)
    slot_rows = (codes.T[:, None, :] == slot_ids[None, :, None]).astype(jnp.bfloat16)
    copies = device_count // expert_count
    dest_rows = jnp.repeat(slot_rows, copies, axis=0) if copies > 1 else slot_rows
    dest_flat = dest_rows.reshape(device_count * cap_pad, rows_own)

    def exchange(blocks):
        return lax.all_to_all(blocks, world, split_axis=0, concat_axis=0, tiled=True)

    def dispatch(rows):
        picked = jnp.dot(dest_flat, rows, preferred_element_type=jnp.float32).astype(jnp.bfloat16)
        arrived = exchange(picked.reshape(device_count, cap_pad, model_width))
        return arrived.reshape(device_count * cap_pad, model_width)

    def combine(blocks):
        returned = exchange(blocks.reshape(device_count, cap_pad, model_width))
        return jnp.dot(
            dest_flat.T,
            returned.reshape(device_count * cap_pad, model_width),
            preferred_element_type=jnp.float32,
        )

    cot_arrived = dispatch(cotangent)

    member, ancestor, positions = jax.vmap(tree_layout)(parents)
    cos_table, sin_table = rope_tables(positions.reshape(-1))
    hidden_f = hidden.astype(jnp.float32)
    unit_one, inverse_one = normalize(hidden_f)
    normed_one = (unit_one * norm_gains[0]).astype(jnp.bfloat16)
    qkv_flat = qkv_weight.reshape(model_width, 3 * local_width)
    qkv_all = jnp.dot(normed_one, qkv_flat, preferred_element_type=jnp.float32)
    query_raw = qkv_all[:, :local_width]
    key_raw = qkv_all[:, local_width : 2 * local_width]
    value_raw = qkv_all[:, 2 * local_width :]
    query_sq, key_sq = lax.psum(
        (jnp.sum(query_raw * query_raw, axis=1), jnp.sum(key_raw * key_raw, axis=1)), "tp"
    )
    query_inv = lax.rsqrt(query_sq / model_width + EPSILON)[:, None]
    key_inv = lax.rsqrt(key_sq / model_width + EPSILON)[:, None]
    query_hat = query_raw * query_inv
    key_hat = key_raw * key_inv
    head_shape = (rows_all, local_heads, HEAD_DIM)
    query_low = rotate((query_hat * qk_gain[0]).reshape(head_shape), cos_table, sin_table).astype(
        jnp.bfloat16
    )
    key_low = rotate((key_hat * qk_gain[1]).reshape(head_shape), cos_table, sin_table).astype(
        jnp.bfloat16
    )
    value_low = value_raw.reshape(head_shape).astype(jnp.bfloat16)
    tree_shape = (tree_count, tree_len, local_heads, HEAD_DIM)
    query_trees = query_low.reshape(tree_shape)
    key_trees = key_low.reshape(tree_shape)
    value_trees = value_low.reshape(tree_shape)
    context_low, log_total = lax.map(
        attend, (query_trees, key_trees, value_trees, member, ancestor, positions)
    )
    context_low = context_low.reshape(rows_all, local_width)
    attention = lax.psum_scatter(
        jnp.dot(context_low, out_weight, preferred_element_type=jnp.float32).astype(jnp.bfloat16),
        "tp",
        scatter_dimension=0,
        tiled=True,
    ).astype(jnp.float32)
    hidden_own = lax.dynamic_slice_in_dim(hidden, own_start, rows_own, 0).astype(jnp.float32)
    mixed = hidden_own + attention
    unit_two, inverse_two = normalize(mixed)
    normed_two = (unit_two * norm_gains[1]).astype(jnp.bfloat16)
    logits = jnp.dot(normed_two, router_weight, preferred_element_type=jnp.float32)
    route_probs = softmax_rows(logits)

    arrived = dispatch(normed_two)
    own_expert = device_rank * half_count // 2
    arrived_probs = softmax_rows(jnp.dot(arrived, router_weight, preferred_element_type=jnp.float32))
    gate = jnp.sum(jnp.where(labels[None, :] == own_expert, arrived_probs, 0.0), axis=1)[:, None]
    gate_up_flat = gate_up.reshape(half_count, model_width, 2 * ff_half)
    pre_act = jnp.einsum("nd,pdf->pnf", arrived, gate_up_flat, preferred_element_type=jnp.float32)
    gate_pre = pre_act[..., :ff_half]
    up_pre = pre_act[..., ff_half:]
    sigmoid_gate = jax.nn.sigmoid(gate_pre)
    hidden_activation = (gate_pre * sigmoid_gate * up_pre).astype(jnp.bfloat16)
    act_raw = jnp.einsum("nd,pfd->pnf", cot_arrived, down_weight, preferred_element_type=jnp.float32)
    gate_dot = jnp.sum(act_raw * hidden_activation.astype(jnp.float32), axis=(0, 2))
    act_grad = act_raw * gate
    gate_grad_pre = act_grad * up_pre * sigmoid_gate * (1.0 + gate_pre * (1.0 - sigmoid_gate))
    up_grad_pre = act_grad * gate_pre * sigmoid_gate
    pre_grad = jnp.concatenate([gate_grad_pre, up_grad_pre], axis=-1).astype(jnp.bfloat16)
    input_part = jnp.einsum(
        "pnf,pdf->nd", pre_grad, gate_up_flat, preferred_element_type=jnp.float32
    ).astype(jnp.bfloat16)
    expert_part = (
        gate
        * jnp.einsum(
            "pnf,pfd->nd", hidden_activation, down_weight, preferred_element_type=jnp.float32
        )
    ).astype(jnp.bfloat16)
    gate_back = exchange(gate_dot.reshape(device_count, cap_pad))
    expert_grad = combine(input_part)
    hidden_gated = (hidden_activation.astype(jnp.float32) * gate).astype(jnp.bfloat16)
    down_grad = jnp.einsum(
        "pnf,nd->pfd", hidden_gated, cot_arrived, preferred_element_type=jnp.float32
    )
    gate_up_grad = jnp.einsum(
        "nd,pnf->pdf", arrived, pre_grad, preferred_element_type=jnp.float32
    ).reshape(half_count, model_width, 2, ff_half)

    gate_back = jnp.sum(gate_back.reshape(expert_count, copies, cap_pad), axis=1)
    prob_grad = jnp.sum(
        jnp.where(codes[:, :, None] == slot_ids[None, None, :], gate_back[None], 0.0), axis=2
    )
    logit_grad = route_probs * (prob_grad - jnp.sum(route_probs * prob_grad, axis=1, keepdims=True))
    logit_low = logit_grad.astype(jnp.bfloat16)
    normed_grad = expert_grad + jnp.dot(
        logit_low, router_weight.T, preferred_element_type=jnp.float32
    )
    router_grad = jnp.dot(normed_two.T, logit_low, preferred_element_type=jnp.float32)
    gain_two_grad = jnp.sum(normed_grad * unit_two, axis=0)
    mixed_grad = cotangent.astype(jnp.float32) + norm_back(
        normed_grad, unit_two, inverse_two, norm_gains[1]
    )
    mixed_low = lax.all_gather(mixed_grad.astype(jnp.bfloat16), "tp", axis=0, tiled=True)
    out_weight_grad = jnp.dot(context_low.T, mixed_low, preferred_element_type=jnp.float32)
    context_grad = jnp.dot(mixed_low, out_weight.T, preferred_element_type=jnp.float32).astype(
        jnp.bfloat16
    )
    out_weight_sum = lax.psum(out_weight_grad.astype(jnp.bfloat16), "exp").astype(jnp.float32)
    query_grad, key_grad, value_grad = lax.map(
        attend_back,
        (
            query_trees,
            key_trees,
            value_trees,
            context_grad.reshape(tree_shape),
            log_total,
            member,
            ancestor,
            positions,
        ),
    )
    query_grad = unrotate(query_grad.reshape(head_shape), cos_table, sin_table).reshape(
        rows_all, local_width
    )
    key_grad = unrotate(key_grad.reshape(head_shape), cos_table, sin_table).reshape(
        rows_all, local_width
    )
    query_gain_grad = jnp.sum(query_grad * query_hat, axis=0)
    key_gain_grad = jnp.sum(key_grad * key_hat, axis=0)
    query_hat_grad = query_grad * qk_gain[0]
    key_hat_grad = key_grad * qk_gain[1]
    query_dot, key_dot = lax.psum(
        (jnp.sum(query_hat_grad * query_hat, axis=1), jnp.sum(key_hat_grad * key_hat, axis=1)), "tp"
    )
    query_raw_grad = query_inv * (query_hat_grad - query_hat * (query_dot / model_width)[:, None])
    key_raw_grad = key_inv * (key_hat_grad - key_hat * (key_dot / model_width)[:, None])
    qkv_grad_low = jnp.concatenate(
        [query_raw_grad, key_raw_grad, value_grad.reshape(rows_all, local_width)], axis=1
    ).astype(jnp.bfloat16)
    normed_one_grad = lax.psum_scatter(
        jnp.dot(qkv_grad_low, qkv_flat.T, preferred_element_type=jnp.float32).astype(jnp.bfloat16),
        "tp",
        scatter_dimension=0,
        tiled=True,
    ).astype(jnp.float32)
    qkv_weight_grad = jnp.dot(
        normed_one.T, qkv_grad_low, preferred_element_type=jnp.float32
    ).reshape(model_width, 3, local_width)
    qkv_sum = lax.psum(qkv_weight_grad.astype(jnp.bfloat16), "exp").astype(jnp.float32)
    unit_own, inverse_own = normalize(hidden_own)
    gain_one_grad = jnp.sum(normed_one_grad * unit_own, axis=0)
    input_grad = lax.all_gather(
        (mixed_grad + norm_back(normed_one_grad, unit_own, inverse_own, norm_gains[0])).astype(
            jnp.bfloat16
        ),
        "tp",
        axis=0,
        tiled=True,
    )
    layer_out = (mixed + combine(expert_part)).astype(jnp.bfloat16)
    qk_sum = lax.psum(jnp.stack([query_gain_grad, key_gain_grad]), "exp")
    gains_sum, router_sum = lax.psum((jnp.stack([gain_one_grad, gain_two_grad]), router_grad), world)
    return (
        layer_out,
        input_grad,
        gains_sum,
        qkv_sum,
        qk_sum,
        out_weight_sum,
        router_sum,
        gate_up_grad,
        down_grad,
    )


def solution(mesh):
    return jax.shard_map(
        shards,
        mesh=mesh,
        in_specs=(
            P("exp", None),
            P(("exp", "tp"), None),
            P(),
            P(None, None, "tp"),
            P(None, "tp"),
            P("tp", None),
            P(),
            P(("exp", "tp"), None, None, None),
            P(("exp", "tp"), None, None),
            P("exp", None),
            P("exp", None),
        ),
        out_specs=(
            P(("exp", "tp"), None),
            P("exp", None),
            P(),
            P(None, None, "tp"),
            P(None, "tp"),
            P("tp", None),
            P(),
            P(("exp", "tp"), None, None, None),
            P(("exp", "tp"), None, None),
        ),
        check_vma=False,
    )
```

```python
import functools

import jax
import jax.numpy as jnp
from jax import lax
from jax.experimental import pallas as pl
from jax.experimental.pallas import tpu as pltpu
from jax.sharding import PartitionSpec as P

HEAD_DIM = 128
TRUNK = 512
BRANCH = 64


EPSILON = 1e-05
BASE_FREQ = 10000.0
MASKED_SCORE = -1e30
VMEM_BYTES = 60 * 1024 * 1024
PRECISE_MATMUL = lax.Precision.HIGHEST


def normalize(tensor):
    inverse = lax.rsqrt(jnp.mean(tensor * tensor, axis=-1, keepdims=True) + EPSILON)
    return (tensor * inverse, inverse)


def norm_back(grad_in, unit, inverse, gain):
    scaled = grad_in * gain
    return inverse * (scaled - unit * jnp.mean(scaled * unit, axis=-1, keepdims=True))


def softmax_rows(scores):
    weights = jnp.exp(scores - jnp.max(scores, axis=-1, keepdims=True))
    return weights / jnp.sum(weights, axis=-1, keepdims=True)


def tree_layout(parent_row):
    row_index = jnp.arange(TRUNK + 12 * BRANCH, dtype=jnp.int32)
    segment = jnp.where(row_index < TRUNK, 0, 1 + (row_index - TRUNK) // BRANCH)
    offset = jnp.where(row_index < TRUNK, row_index, (row_index - TRUNK) % BRANCH)
    branch = parent_row == 0
    branch_order = jnp.cumsum(branch.astype(jnp.int32))
    leaf_link = (
        (parent_row[:, None] == branch_order[None, :])
        & branch[None, :]
        & jnp.logical_not(branch)[:, None]
    )
    parent = jnp.zeros((13, 13), jnp.float32)
    parent = parent.at[1:, 0].set(branch.astype(jnp.float32))
    parent = parent.at[1:, 1:].set(leaf_link.astype(jnp.float32))
    ancestor = (
        jnp.eye(13, dtype=jnp.float32) + parent + jnp.dot(parent, parent, precision=PRECISE_MATMUL)
    )
    depth_table = jnp.concatenate(
        [jnp.zeros((1,), jnp.int32), jnp.where(branch, 1, 2).astype(jnp.int32)]
    )
    labels = jnp.arange(13, dtype=jnp.int32)
    member = segment[:, None] == labels[None, :]
    depth_rank = jnp.sum(jnp.where(member, depth_table[None, :], 0), axis=1)
    positions = (
        offset + jnp.where(depth_rank >= 1, TRUNK, 0) + jnp.where(depth_rank == 2, BRANCH, 0)
    )
    return (member.astype(jnp.float32), ancestor, positions)


def path_mask(member, ancestor, positions):
    reached_slots = jnp.dot(
        jnp.dot(member, ancestor, precision=PRECISE_MATMUL), member.T, precision=PRECISE_MATMUL
    )
    return (reached_slots > 0.5) & (positions[None, :] <= positions[:, None])


def rope_tables(positions):
    frequency = BASE_FREQ ** (-jnp.arange(0, HEAD_DIM, 2, dtype=jnp.float32) / HEAD_DIM)
    angles = positions.astype(jnp.float32)[:, None] * frequency[None, :]
    cos_half = jnp.cos(angles)
    sin_half = jnp.sin(angles)
    return (
        jnp.concatenate([cos_half, cos_half], axis=-1),
        jnp.concatenate([sin_half, sin_half], axis=-1),
    )


def rotate(tensor, cos_table, sin_table):
    half_dim = tensor.shape[-1] // 2
    turned = jnp.concatenate([-tensor[..., half_dim:], tensor[..., :half_dim]], axis=-1)
    return tensor * cos_table[:, None, :] + turned * sin_table[:, None, :]


def unrotate(tensor, cos_table, sin_table):
    half_dim = tensor.shape[-1] // 2
    shifted = tensor * sin_table[:, None, :]
    return tensor * cos_table[:, None, :] + jnp.concatenate(
        [shifted[..., half_dim:], -shifted[..., :half_dim]], axis=-1
    )


def scores_of(query_tree, key_tree, member, ancestor, positions):
    allowed = path_mask(member, ancestor, positions)
    raw = jnp.einsum(
        "qhd,khd->hqk", query_tree, key_tree, preferred_element_type=jnp.float32
    ) * HEAD_DIM ** (-0.5)
    return jnp.where(allowed[None], raw, MASKED_SCORE)


def attend(tree_block):
    query_tree, key_tree, value_tree, member, ancestor, positions = tree_block
    scores = scores_of(query_tree, key_tree, member, ancestor, positions)
    top_score = jnp.max(scores, axis=2, keepdims=True)
    weights = jnp.exp(scores - top_score)
    total = jnp.sum(weights, axis=2, keepdims=True)
    attn_probs = weights / total
    context = jnp.einsum(
        "hqk,khd->qhd",
        attn_probs.astype(jnp.bfloat16),
        value_tree,
        preferred_element_type=jnp.float32,
    )
    return (context.astype(jnp.bfloat16), top_score[..., 0] + jnp.log(total[..., 0]))


def attend_back(tree_block):
    query_tree, key_tree, value_tree, context_grad, log_total, member, ancestor, positions = (
        tree_block
    )
    scores = scores_of(query_tree, key_tree, member, ancestor, positions)
    attn_probs = jnp.exp(scores - log_total[..., None])
    prob_grad = jnp.einsum(
        "qhd,khd->hqk", context_grad, value_tree, preferred_element_type=jnp.float32
    )
    score_grad = attn_probs * (prob_grad - jnp.sum(attn_probs * prob_grad, axis=2, keepdims=True))
    score_low = score_grad.astype(jnp.bfloat16)
    scale = HEAD_DIM ** (-0.5)
    query_grad = (
        jnp.einsum("hqk,khd->qhd", score_low, key_tree, preferred_element_type=jnp.float32) * scale
    )
    key_grad = (
        jnp.einsum("hqk,qhd->khd", score_low, query_tree, preferred_element_type=jnp.float32)
        * scale
    )
    value_grad = jnp.einsum(
        "hqk,qhd->khd",
        attn_probs.astype(jnp.bfloat16),
        context_grad,
        preferred_element_type=jnp.float32,
    )
    return (query_grad, key_grad, value_grad)


MESH_ID = pl.DeviceIdType.MESH


def flip(index, step):
    if step == 0:
        return index
    if step == 1:
        return index + 1 - 2 * lax.rem(index, 2)
    if step == 2:
        return lax.rem(index + 2, 4)
    return 3 - index


def places(lo_count, tp_count):
    hi, lo, tp = lax.axis_index("hi"), lax.axis_index("lo"), lax.axis_index("tp")

    def along(step):
        return {"hi": flip(hi, step), "lo": lo, "tp": tp}

    def across(q):
        return {"hi": hi, "lo": q // tp_count, "tp": lax.rem(q, tp_count)}

    return hi, lo * tp_count + tp, along, across


def greet(plane, me, along, across):
    barrier = pltpu.get_barrier_semaphore()
    for step in range(1, 4):
        pl.semaphore_signal(barrier, inc=1, device_id=along(step), device_id_type=MESH_ID)

    def one(q, carry):
        @pl.when(q != me)
        def _():
            pl.semaphore_signal(barrier, inc=1, device_id=across(q), device_id_type=MESH_ID)

        return carry

    lax.fori_loop(0, plane, one, 0)
    pl.semaphore_wait(barrier, 3 + plane - 1)


def wait_bytes(ref, sem):
    pltpu.make_async_copy(ref, ref, sem).wait()


def spread_kernel(
    lo_count,
    tp_count,
    cap_pad,
    half_count,
    rows_ref,
    pick_ref,
    router_ref,
    gate_up_ref,
    arrived_ref,
    pre_ref,
    gate_ref,
    far_ref,
    send_ref,
    chunk_ref,
    weight_ref,
    out_ref,
    far_send,
    far_recv,
    near_send,
    near_recv,
    own_sem,
    load_sem,
    weight_sem,
    out_sem,
):
    plane = lo_count * tp_count
    hi, me, along, across = places(lo_count, tp_count)
    count = plane * cap_pad
    width = rows_ref.shape[1]
    wide = gate_up_ref.shape[2]
    fill = pltpu.make_async_copy(gate_up_ref, weight_ref, weight_sem)
    fill.start()
    greet(plane, me, along, across)

    def far_copy(step):
        return pltpu.make_async_remote_copy(
            src_ref=rows_ref,
            dst_ref=far_ref.at[step - 1],
            send_sem=far_send.at[step - 1],
            recv_sem=far_recv.at[step - 1],
            device_id=along(step),
            device_id_type=MESH_ID,
        )

    def near_copy(step, slot, q):
        return pltpu.make_async_remote_copy(
            src_ref=send_ref.at[slot, pl.ds(pl.multiple_of(q * cap_pad, 16), cap_pad)],
            dst_ref=arrived_ref.at[step, pl.ds(pl.multiple_of(me * cap_pad, 16), cap_pad)],
            send_sem=near_send.at[step],
            recv_sem=near_recv.at[step],
            device_id=across(q),
            device_id_type=MESH_ID,
        )

    def own_copy(step, slot):
        return pltpu.make_async_copy(
            send_ref.at[slot, pl.ds(pl.multiple_of(me * cap_pad, 16), cap_pad)],
            arrived_ref.at[step, pl.ds(pl.multiple_of(me * cap_pad, 16), cap_pad)],
            own_sem.at[step],
        )

    others = pl.ds(0, count - cap_pad)

    def sent(step):
        wait_bytes(send_ref.at[step % 2, others], near_send.at[step])

    def select(step):
        slot = step % 2
        if step >= 2:
            sent(step - 2)

        def one(turn, carry):
            q = lax.rem(me + 1 + turn, plane)
            start = pl.multiple_of(q * cap_pad, 16)
            rows = rows_ref[...] if step == 0 else far_ref[step - 1]
            picked = jnp.dot(
                pick_ref[step, pl.ds(start, cap_pad)], rows, preferred_element_type=jnp.float32
            )
            send_ref[slot, pl.ds(start, cap_pad)] = picked.astype(jnp.bfloat16)

            @pl.when(q != me)
            def _():
                near_copy(step, slot, q).start()

            @pl.when(q == me)
            def _():
                own_copy(step, slot).start()

            return carry

        lax.fori_loop(0, plane, one, 0)

    def out_copy(step):
        return pltpu.make_async_copy(out_ref.at[step % 2], pre_ref.at[step], out_sem.at[step % 2])

    def forward(step):
        wait_bytes(arrived_ref.at[step, others], near_recv.at[step])
        own_copy(step, step % 2).wait()
        load = pltpu.make_async_copy(arrived_ref.at[step], chunk_ref, load_sem)
        load.start()
        load.wait()
        logits = jnp.dot(chunk_ref[...], router_ref[...], preferred_element_type=jnp.float32)
        weights = jnp.exp(logits - jnp.max(logits, axis=1, keepdims=True))
        own_expert = (hi * plane + me) * half_count // 2
        lanes = lax.broadcasted_iota(jnp.int32, weights.shape, 1)
        own = jnp.sum(jnp.where(lanes == own_expert, weights, 0.0), axis=1, keepdims=True)
        gate_ref[step] = own / jnp.sum(weights, axis=1, keepdims=True)
        if step == 0:
            fill.wait()
        if step >= 2:
            out_copy(step - 2).wait()
        tile = 256

        def one(index, carry):
            half = index // (wide // tile)
            start = pl.multiple_of(lax.rem(index, wide // tile) * tile, tile)
            out = jnp.dot(
                chunk_ref[...],
                weight_ref[half, :, pl.ds(start, tile)],
                preferred_element_type=jnp.float32,
            )
            out_ref[step % 2, :, pl.ds(pl.multiple_of(index * tile, tile), tile)] = out.astype(
                jnp.bfloat16
            )
            return carry

        lax.fori_loop(0, half_count * (wide // tile), one, 0)
        out_copy(step).start()

    far_copy(1).start()
    far_copy(2).start()
    select(0)
    far_copy(1).wait_recv()
    select(1)
    forward(0)
    far_copy(2).wait_recv()
    far_copy(3).start()
    select(2)
    forward(1)
    far_copy(3).wait_recv()
    select(3)
    forward(2)
    forward(3)
    for step in (2, 3):
        sent(step)
        out_copy(step).wait()
    for step in (1, 2, 3):
        far_copy(step).wait_send()


def spread(lo_count, tp_count, cap_pad, half_count, rows, pick, router, gate_up):
    plane = lo_count * tp_count
    count = plane * cap_pad
    width = rows.shape[1]
    wide = half_count * gate_up.shape[2]
    whole = pl.BlockSpec(memory_space=pltpu.VMEM)
    anywhere = pl.BlockSpec(memory_space=pl.ANY)
    return pl.pallas_call(
        functools.partial(spread_kernel, lo_count, tp_count, cap_pad, half_count),
        out_shape=(
            jax.ShapeDtypeStruct((4, count, width), jnp.bfloat16),
            jax.ShapeDtypeStruct((4, count, wide), jnp.bfloat16),
            jax.ShapeDtypeStruct((4, count, 1), jnp.float32),
        ),
        in_specs=[whole, whole, whole, anywhere],
        out_specs=(anywhere, anywhere, whole),
        scratch_shapes=[
            pltpu.VMEM((3,) + rows.shape, jnp.bfloat16),
            pltpu.VMEM((2, count, width), jnp.bfloat16),
            pltpu.VMEM((count, width), jnp.bfloat16),
            pltpu.VMEM(gate_up.shape, jnp.bfloat16),
            pltpu.VMEM((2, count, wide), jnp.bfloat16),
            pltpu.SemaphoreType.DMA((3,)),
            pltpu.SemaphoreType.DMA((3,)),
            pltpu.SemaphoreType.DMA((4,)),
            pltpu.SemaphoreType.DMA((4,)),
            pltpu.SemaphoreType.DMA((4,)),
            pltpu.SemaphoreType.DMA,
            pltpu.SemaphoreType.DMA,
            pltpu.SemaphoreType.DMA((2,)),
        ],
        compiler_params=pltpu.CompilerParams(
            collective_id=1, has_side_effects=True, vmem_limit_bytes=VMEM_BYTES
        ),
        cost_estimate=pl.CostEstimate(
            flops=8 * count * width * (wide + rows.shape[0]),
            bytes_accessed=16 * count * width,
            transcendentals=0,
        ),
    )(rows, pick, router, gate_up)


def gather_kernel(
    lo_count,
    tp_count,
    cap_pad,
    half_count,
    pre_ref,
    cot_ref,
    gate_ref,
    gate_up_hbm,
    down_hbm,
    back_ref,
    grad_ref,
    dot_ref,
    low_ref,
    hidden_ref,
    land_ref,
    pre_buf,
    cot_buf,
    gate_up_ref,
    down_ref,
    low_buf,
    hidden_buf,
    send_ref,
    land_buf,
    part_ref,
    home_ref,
    weight_sem,
    load_sem,
    store_sem,
    near_send,
    near_recv,
    own_sem,
    land_sem,
    far_send,
    far_recv,
):
    plane = lo_count * tp_count
    hi, me, along, across = places(lo_count, tp_count)
    count = plane * cap_pad
    width = cot_ref.shape[2]
    ff_half = gate_up_ref.shape[2] // 2
    fill_down = pltpu.make_async_copy(down_hbm, down_ref, weight_sem.at[0])
    fill_gate_up = pltpu.make_async_copy(gate_up_hbm, gate_up_ref, weight_sem.at[1])
    order = (3, 2, 1, 0)

    def loads(step):
        return (
            pltpu.make_async_copy(pre_ref.at[step], pre_buf, load_sem.at[0]),
            pltpu.make_async_copy(cot_ref.at[step], cot_buf, load_sem.at[1]),
        )

    def stores(step):
        return (
            pltpu.make_async_copy(low_buf, low_ref.at[step], store_sem.at[0]),
            pltpu.make_async_copy(hidden_buf, hidden_ref.at[step], store_sem.at[1]),
        )

    fill_down.start()
    for copy in loads(order[0]):
        copy.start()
    fill_gate_up.start()
    greet(plane, me, along, across)

    def block(q):
        return pl.ds(pl.multiple_of(q * cap_pad, 16), cap_pad)

    others = pl.ds(0, count - cap_pad)

    def near_copy(step, q):
        return pltpu.make_async_remote_copy(
            src_ref=send_ref.at[step % 2, block(q)],
            dst_ref=land_ref.at[step, block(me)],
            send_sem=near_send.at[step],
            recv_sem=near_recv.at[step],
            device_id=across(q),
            device_id_type=MESH_ID,
        )

    def own_copy(step):
        return pltpu.make_async_copy(
            send_ref.at[step % 2, block(me)], land_ref.at[step, block(me)], own_sem.at[step]
        )

    def far_copy(step):
        return pltpu.make_async_remote_copy(
            src_ref=part_ref.at[step - 1],
            dst_ref=home_ref.at[step - 1],
            send_sem=far_send.at[step - 1],
            recv_sem=far_recv.at[step - 1],
            device_id=along(step),
            device_id_type=MESH_ID,
        )

    def backward(turn):
        step = order[turn]
        if turn == 0:
            fill_down.wait()
        for copy in loads(step):
            copy.wait()
        if turn > 0:
            for copy in stores(order[turn - 1]):
                copy.wait()
        dot_ref[step] = jnp.zeros(dot_ref.shape[1:], jnp.float32)
        tile = 256

        def act(index, carry):
            half = index // (ff_half // tile)
            inner = lax.rem(index, ff_half // tile) * tile
            gate_at = pl.ds(pl.multiple_of(half * 2 * ff_half + inner, tile), tile)
            up_at = pl.ds(pl.multiple_of(half * 2 * ff_half + ff_half + inner, tile), tile)
            unit_at = pl.ds(pl.multiple_of(index * tile, tile), tile)
            raw = lax.dot_general(
                cot_buf[...],
                down_ref[unit_at, :],
                (((1,), (1,)), ((), ())),
                preferred_element_type=jnp.float32,
            )
            gate_pre = pre_buf[:, gate_at].astype(jnp.float32)
            up_pre = pre_buf[:, up_at].astype(jnp.float32)
            gate = gate_ref[step]
            sigmoid = 1.0 / (1.0 + jnp.exp(-gate_pre))
            swish = gate_pre * sigmoid
            hidden = swish * up_pre
            dot_ref[step] += jnp.sum(raw * hidden, axis=1, keepdims=True)
            hidden_buf[:, unit_at] = (hidden * gate).astype(jnp.bfloat16)
            act_grad = raw * gate
            low_buf[:, gate_at] = (
                act_grad * up_pre * (sigmoid + swish * (1.0 - sigmoid))
            ).astype(jnp.bfloat16)
            low_buf[:, up_at] = (act_grad * swish).astype(jnp.bfloat16)
            return carry

        lax.fori_loop(0, half_count * (ff_half // tile), act, 0)
        for copy in stores(step):
            copy.start()
        if turn < 3:
            for copy in loads(order[turn + 1]):
                copy.start()
        if turn == 0:
            fill_gate_up.wait()
        if turn >= 2:
            wait_bytes(send_ref.at[step % 2, others], near_send.at[order[turn - 2]])
            own_copy(order[turn - 2]).wait()

        def down(index, carry):
            at = pl.ds(pl.multiple_of(index * tile, tile), tile)
            total = None
            for half in range(half_count):
                part = lax.dot_general(
                    low_buf[:, half * 2 * ff_half : (half + 1) * 2 * ff_half],
                    gate_up_ref[half, at, :],
                    (((1,), (1,)), ((), ())),
                    preferred_element_type=jnp.float32,
                )
                total = part if total is None else total + part
            send_ref[step % 2, :, at] = total.astype(jnp.bfloat16)
            return carry

        lax.fori_loop(0, width // tile, down, 0)

        def send(turn_q, carry):
            q = lax.rem(me + 1 + turn_q, plane)

            @pl.when(q != me)
            def _():
                near_copy(step, q).start()

            @pl.when(q == me)
            def _():
                own_copy(step).start()

            return carry

        lax.fori_loop(0, plane, send, 0)

    def merge(step):
        wait_bytes(land_ref.at[step, others], near_recv.at[step])
        if step < 2:
            own_copy(step).wait()
        load = pltpu.make_async_copy(land_ref.at[step], land_buf, land_sem)
        load.start()
        load.wait()
        tile = 512

        def one(index, carry):
            at = pl.ds(pl.multiple_of(index * tile, tile), tile)
            total = jnp.dot(back_ref[step], land_buf[:, at], preferred_element_type=jnp.float32)
            if step == 0:
                for far in range(3):
                    total = total + home_ref[far, :, at].astype(jnp.float32)
                grad_ref[:, at] = total
            else:
                part_ref[step - 1, :, at] = total.astype(jnp.bfloat16)
            return carry

        if step == 0:
            for far in (1, 2, 3):
                far_copy(far).wait_recv()
        lax.fori_loop(0, width // tile, one, 0)
        if step > 0:
            far_copy(step).start()

    backward(0)
    backward(1)
    backward(2)
    merge(3)
    backward(3)
    merge(2)
    merge(1)
    merge(0)
    for copy in stores(0):
        copy.wait()
    for step in (1, 0):
        wait_bytes(send_ref.at[step % 2, others], near_send.at[step])
    for step in (1, 2, 3):
        far_copy(step).wait_send()


def gather(lo_count, tp_count, cap_pad, half_count, pre, cot, gate, gate_up, down, back):
    plane = lo_count * tp_count
    count = plane * cap_pad
    width = cot.shape[2]
    wide = pre.shape[2]
    units = down.shape[0]
    rows = back.shape[1]
    whole = pl.BlockSpec(memory_space=pltpu.VMEM)
    anywhere = pl.BlockSpec(memory_space=pl.ANY)
    return pl.pallas_call(
        functools.partial(gather_kernel, lo_count, tp_count, cap_pad, half_count),
        out_shape=(
            jax.ShapeDtypeStruct((rows, width), jnp.float32),
            jax.ShapeDtypeStruct((4, count, 1), jnp.float32),
            jax.ShapeDtypeStruct((4, count, wide), jnp.bfloat16),
            jax.ShapeDtypeStruct((4, count, units), jnp.bfloat16),
            jax.ShapeDtypeStruct((4, count, width), jnp.bfloat16),
        ),
        in_specs=[anywhere, anywhere, whole, anywhere, anywhere, whole],
        out_specs=(whole, whole, anywhere, anywhere, anywhere),
        scratch_shapes=[
            pltpu.VMEM((count, wide), jnp.bfloat16),
            pltpu.VMEM((count, width), jnp.bfloat16),
            pltpu.VMEM(gate_up.shape, jnp.bfloat16),
            pltpu.VMEM(down.shape, jnp.bfloat16),
            pltpu.VMEM((count, wide), jnp.bfloat16),
            pltpu.VMEM((count, units), jnp.bfloat16),
            pltpu.VMEM((2, count, width), jnp.bfloat16),
            pltpu.VMEM((count, width), jnp.bfloat16),
            pltpu.VMEM((3, rows, width), jnp.bfloat16),
            pltpu.VMEM((3, rows, width), jnp.bfloat16),
            pltpu.SemaphoreType.DMA((2,)),
            pltpu.SemaphoreType.DMA((2,)),
            pltpu.SemaphoreType.DMA((2,)),
            pltpu.SemaphoreType.DMA((4,)),
            pltpu.SemaphoreType.DMA((4,)),
            pltpu.SemaphoreType.DMA((4,)),
            pltpu.SemaphoreType.DMA,
            pltpu.SemaphoreType.DMA((3,)),
            pltpu.SemaphoreType.DMA((3,)),
        ],
        compiler_params=pltpu.CompilerParams(
            collective_id=2, has_side_effects=True, vmem_limit_bytes=VMEM_BYTES
        ),
        cost_estimate=pl.CostEstimate(
            flops=24 * count * width * units,
            bytes_accessed=16 * count * width,
            transcendentals=0,
        ),
    )(pre, cot, gate, gate_up, down, back)


def shards(
    hidden,
    cotangent,
    norm_gains,
    qkv_weight,
    qk_gain,
    out_weight,
    router_weight,
    gate_up,
    down_weight,
    routes,
    parents,
):
    tp_count = lax.axis_size("tp")
    hi_count = lax.axis_size("hi")
    lo_count = lax.axis_size("lo")
    tp_rank = lax.axis_index("tp")
    hi_rank = lax.axis_index("hi")
    exp = ("hi", "lo")
    world = ("hi", "lo", "tp")
    plane = lo_count * tp_count
    device_count = hi_count * plane
    rows_all, model_width = hidden.shape
    rows_own = cotangent.shape[0]
    local_width = qkv_weight.shape[2]
    local_heads = local_width // HEAD_DIM
    expert_count = router_weight.shape[1]
    half_count = gate_up.shape[0]
    ff_half = gate_up.shape[3]
    top_count = routes.shape[1]
    capacity = (9 * rows_own * top_count + 8 * expert_count - 1) // (8 * expert_count)
    cap_pad = -(-capacity // 16) * 16
    tree_count = parents.shape[0]
    tree_len = rows_all // tree_count
    own_start = tp_rank * rows_own

    own_routes = lax.dynamic_slice_in_dim(routes, own_start, rows_own, 0)
    labels = jnp.arange(expert_count, dtype=jnp.int32)
    hits = jnp.any(own_routes[:, :, None] == labels[None, None, :], axis=1)
    row_ids = jnp.arange(rows_own, dtype=jnp.int32)
    earlier = (row_ids[:, None] > row_ids[None, :]).astype(jnp.bfloat16)
    slots = jnp.dot(earlier, hits.astype(jnp.bfloat16), preferred_element_type=jnp.float32).astype(
        jnp.int32
    )
    kept = hits & (slots < capacity)
    codes = jnp.where(kept, slots, -1)
    copies = device_count // expert_count
    near_count = plane // copies
    chunk_ids = hi_rank ^ jnp.arange(hi_count, dtype=jnp.int32)
    codes_all = lax.all_gather(codes.astype(jnp.float32), "hi", axis=0, tiled=False)
    near_codes = lax.dynamic_slice_in_dim(codes_all, hi_rank * near_count, near_count, 2)
    near_codes = jnp.take(near_codes, chunk_ids, axis=0).astype(jnp.int32)
    if copies > 1:
        near_codes = jnp.repeat(near_codes, copies, axis=2)
    slot_ids = jnp.arange(cap_pad, dtype=jnp.int32)
    pick = (
        (near_codes.transpose(0, 2, 1)[:, :, None, :] == slot_ids[None, None, :, None])
        .astype(jnp.bfloat16)
        .reshape(hi_count, plane * cap_pad, rows_own)
    )
    back = (
        (near_codes[:, :, :, None] == slot_ids[None, None, None, :])
        .astype(jnp.bfloat16)
        .reshape(hi_count, rows_own, plane * cap_pad)
    )

    def along(block, step):
        return lax.ppermute(block, "hi", [(i, i ^ step) for i in range(hi_count)])

    def across(block):
        moved = lax.all_to_all(
            block.reshape(plane, cap_pad, model_width),
            ("lo", "tp"),
            split_axis=0,
            concat_axis=0,
            tiled=True,
        )
        return moved.reshape(plane * cap_pad, model_width)

    cot_arrived = []
    cot_slices = [cotangent] + [along(cotangent, step) for step in range(1, hi_count)]
    for step in range(hi_count):
        picked = jnp.dot(pick[step], cot_slices[step], preferred_element_type=jnp.float32)
        cot_arrived.append(across(picked.astype(jnp.bfloat16)))
    cot_arrived = jnp.stack(cot_arrived)

    member, ancestor, positions = jax.vmap(tree_layout)(parents)
    cos_table, sin_table = rope_tables(positions.reshape(-1))
    hidden_f = hidden.astype(jnp.float32)
    unit_one, inverse_one = normalize(hidden_f)
    normed_one = (unit_one * norm_gains[0]).astype(jnp.bfloat16)
    qkv_flat = qkv_weight.reshape(model_width, 3 * local_width)
    qkv_all = jnp.dot(normed_one, qkv_flat, preferred_element_type=jnp.float32)
    query_raw = qkv_all[:, :local_width]
    key_raw = qkv_all[:, local_width : 2 * local_width]
    value_raw = qkv_all[:, 2 * local_width :]
    query_sq, key_sq = lax.psum(
        (jnp.sum(query_raw * query_raw, axis=1), jnp.sum(key_raw * key_raw, axis=1)), "tp"
    )
    query_inv = lax.rsqrt(query_sq / model_width + EPSILON)[:, None]
    key_inv = lax.rsqrt(key_sq / model_width + EPSILON)[:, None]
    query_hat = query_raw * query_inv
    key_hat = key_raw * key_inv
    head_shape = (rows_all, local_heads, HEAD_DIM)
    query_low = rotate((query_hat * qk_gain[0]).reshape(head_shape), cos_table, sin_table).astype(
        jnp.bfloat16
    )
    key_low = rotate((key_hat * qk_gain[1]).reshape(head_shape), cos_table, sin_table).astype(
        jnp.bfloat16
    )
    value_low = value_raw.reshape(head_shape).astype(jnp.bfloat16)
    tree_shape = (tree_count, tree_len, local_heads, HEAD_DIM)
    query_trees = query_low.reshape(tree_shape)
    key_trees = key_low.reshape(tree_shape)
    value_trees = value_low.reshape(tree_shape)
    context_low, log_total = lax.map(
        attend, (query_trees, key_trees, value_trees, member, ancestor, positions)
    )
    context_low = context_low.reshape(rows_all, local_width)
    attention = lax.psum_scatter(
        jnp.dot(context_low, out_weight, preferred_element_type=jnp.float32).astype(jnp.bfloat16),
        "tp",
        scatter_dimension=0,
        tiled=True,
    ).astype(jnp.float32)
    hidden_own = lax.dynamic_slice_in_dim(hidden, own_start, rows_own, 0).astype(jnp.float32)
    mixed = hidden_own + attention
    unit_two, inverse_two = normalize(mixed)
    normed_two = (unit_two * norm_gains[1]).astype(jnp.bfloat16)
    logits = jnp.dot(normed_two, router_weight, preferred_element_type=jnp.float32)
    route_probs = softmax_rows(logits)

    gate_up_flat = gate_up.reshape(half_count, model_width, 2 * ff_half)
    down_flat = down_weight.reshape(half_count * ff_half, model_width)
    sizes = (lo_count, tp_count, cap_pad, half_count)
    arrived, pre_act, gate = spread(*sizes, normed_two, pick, router_weight, gate_up_flat)
    expert_grad, gate_dot, pre_grad, hidden_gated, _ = gather(
        *sizes, pre_act, cot_arrived, gate, gate_up_flat, down_flat, back
    )
    slot_count = hi_count * plane * cap_pad
    gate_back = jnp.take(gate_dot.reshape(hi_count, plane, cap_pad), chunk_ids, axis=0)
    gate_back = lax.all_to_all(
        gate_back.reshape(device_count, cap_pad), world, split_axis=0, concat_axis=0, tiled=True
    )
    expert_part = [
        jnp.dot(hidden_gated[step], down_flat, preferred_element_type=jnp.float32).astype(
            jnp.bfloat16
        )
        for step in range(hi_count)
    ]
    hidden_flat = hidden_gated.reshape(slot_count, half_count * ff_half)
    cot_flat = cot_arrived.reshape(slot_count, model_width)
    down_grad = lax.dot_general(
        hidden_flat, cot_flat, (((0,), (0,)), ((), ())), preferred_element_type=jnp.float32
    ).reshape(half_count, ff_half, model_width)
    gate_up_grad = jnp.einsum(
        "nd,npf->pdf",
        arrived.reshape(slot_count, model_width),
        pre_grad.reshape(slot_count, half_count, 2 * ff_half),
        preferred_element_type=jnp.float32,
    ).reshape(half_count, model_width, 2, ff_half)

    gate_back = jnp.sum(gate_back.reshape(expert_count, copies, cap_pad), axis=1)
    prob_grad = jnp.sum(
        jnp.where(codes[:, :, None] == slot_ids[None, None, :], gate_back[None], 0.0), axis=2
    )
    logit_grad = route_probs * (prob_grad - jnp.sum(route_probs * prob_grad, axis=1, keepdims=True))
    logit_low = logit_grad.astype(jnp.bfloat16)
    normed_grad = expert_grad + jnp.dot(
        logit_low, router_weight.T, preferred_element_type=jnp.float32
    )
    router_grad = jnp.dot(normed_two.T, logit_low, preferred_element_type=jnp.float32)
    gain_two_grad = jnp.sum(normed_grad * unit_two, axis=0)
    mixed_grad = cotangent.astype(jnp.float32) + norm_back(
        normed_grad, unit_two, inverse_two, norm_gains[1]
    )
    mixed_low = lax.all_gather(mixed_grad.astype(jnp.bfloat16), "tp", axis=0, tiled=True)
    out_weight_grad = jnp.dot(context_low.T, mixed_low, preferred_element_type=jnp.float32)
    context_grad = jnp.dot(mixed_low, out_weight.T, preferred_element_type=jnp.float32).astype(
        jnp.bfloat16
    )
    out_weight_sum = lax.psum(out_weight_grad.astype(jnp.bfloat16), exp).astype(jnp.float32)
    query_grad, key_grad, value_grad = lax.map(
        attend_back,
        (
            query_trees,
            key_trees,
            value_trees,
            context_grad.reshape(tree_shape),
            log_total,
            member,
            ancestor,
            positions,
        ),
    )
    query_grad = unrotate(query_grad.reshape(head_shape), cos_table, sin_table).reshape(
        rows_all, local_width
    )
    key_grad = unrotate(key_grad.reshape(head_shape), cos_table, sin_table).reshape(
        rows_all, local_width
    )
    query_gain_grad = jnp.sum(query_grad * query_hat, axis=0)
    key_gain_grad = jnp.sum(key_grad * key_hat, axis=0)
    query_hat_grad = query_grad * qk_gain[0]
    key_hat_grad = key_grad * qk_gain[1]
    query_dot, key_dot = lax.psum(
        (jnp.sum(query_hat_grad * query_hat, axis=1), jnp.sum(key_hat_grad * key_hat, axis=1)), "tp"
    )
    query_raw_grad = query_inv * (query_hat_grad - query_hat * (query_dot / model_width)[:, None])
    key_raw_grad = key_inv * (key_hat_grad - key_hat * (key_dot / model_width)[:, None])
    qkv_grad_low = jnp.concatenate(
        [query_raw_grad, key_raw_grad, value_grad.reshape(rows_all, local_width)], axis=1
    ).astype(jnp.bfloat16)
    normed_one_grad = lax.psum_scatter(
        jnp.dot(qkv_grad_low, qkv_flat.T, preferred_element_type=jnp.float32).astype(jnp.bfloat16),
        "tp",
        scatter_dimension=0,
        tiled=True,
    ).astype(jnp.float32)
    qkv_weight_grad = jnp.dot(
        normed_one.T, qkv_grad_low, preferred_element_type=jnp.float32
    ).reshape(model_width, 3, local_width)
    qkv_sum = lax.psum(qkv_weight_grad.astype(jnp.bfloat16), exp).astype(jnp.float32)
    unit_own, inverse_own = normalize(hidden_own)
    gain_one_grad = jnp.sum(normed_one_grad * unit_own, axis=0)
    input_grad = lax.all_gather(
        (mixed_grad + norm_back(normed_one_grad, unit_own, inverse_own, norm_gains[0])).astype(
            jnp.bfloat16
        ),
        "tp",
        axis=0,
        tiled=True,
    )
    expert_sum = mixed
    for step in reversed(range(hi_count)):
        merged = jnp.dot(back[step], across(expert_part[step]), preferred_element_type=jnp.float32)
        if step > 0:
            merged = along(merged.astype(jnp.bfloat16), step).astype(jnp.float32)
        expert_sum = expert_sum + merged
    layer_out = expert_sum.astype(jnp.bfloat16)
    qk_sum = lax.psum(jnp.stack([query_gain_grad, key_gain_grad]), exp)
    gains_sum, router_sum = lax.psum((jnp.stack([gain_one_grad, gain_two_grad]), router_grad), world)
    return (
        layer_out,
        input_grad,
        gains_sum,
        qkv_sum,
        qk_sum,
        out_weight_sum,
        router_sum,
        gate_up_grad,
        down_grad,
    )


def solution(mesh):
    exp_count, tp_count = mesh.devices.shape
    split = jax.sharding.Mesh(
        mesh.devices.reshape(4, exp_count // 4, tp_count), ("hi", "lo", "tp")
    )
    exp = ("hi", "lo")
    return jax.shard_map(
        shards,
        mesh=split,
        in_specs=(
            P(exp, None),
            P(("hi", "lo", "tp"), None),
            P(),
            P(None, None, "tp"),
            P(None, "tp"),
            P("tp", None),
            P(),
            P(("hi", "lo", "tp"), None, None, None),
            P(("hi", "lo", "tp"), None, None),
            P(exp, None),
            P(exp, None),
        ),
        out_specs=(
            P(("hi", "lo", "tp"), None),
            P(exp, None),
            P(),
            P(None, None, "tp"),
            P(None, "tp"),
            P("tp", None),
            P(),
            P(("hi", "lo", "tp"), None, None, None),
            P(("hi", "lo", "tp"), None, None),
        ),
        check_vma=False,
    )
```

```python
import functools

import jax
import jax.numpy as jnp
from jax import lax
from jax.experimental import pallas as pl
from jax.experimental.pallas import tpu as pltpu
from jax.sharding import PartitionSpec as P

HEAD_DIM = 128
TRUNK = 512
BRANCH = 64


EPSILON = 1e-05
BASE_FREQ = 10000.0
MASKED_SCORE = -1e30
VMEM_BYTES = 60 * 1024 * 1024
PRECISE_MATMUL = lax.Precision.HIGHEST


def normalize(tensor):
    inverse = lax.rsqrt(jnp.mean(tensor * tensor, axis=-1, keepdims=True) + EPSILON)
    return (tensor * inverse, inverse)


def norm_back(grad_in, unit, inverse, gain):
    scaled = grad_in * gain
    return inverse * (scaled - unit * jnp.mean(scaled * unit, axis=-1, keepdims=True))


def softmax_rows(scores):
    weights = jnp.exp(scores - jnp.max(scores, axis=-1, keepdims=True))
    return weights / jnp.sum(weights, axis=-1, keepdims=True)


def tree_layout(parent_row):
    row_index = jnp.arange(TRUNK + 12 * BRANCH, dtype=jnp.int32)
    segment = jnp.where(row_index < TRUNK, 0, 1 + (row_index - TRUNK) // BRANCH)
    offset = jnp.where(row_index < TRUNK, row_index, (row_index - TRUNK) % BRANCH)
    branch = parent_row == 0
    branch_order = jnp.cumsum(branch.astype(jnp.int32))
    leaf_link = (
        (parent_row[:, None] == branch_order[None, :])
        & branch[None, :]
        & jnp.logical_not(branch)[:, None]
    )
    parent = jnp.zeros((13, 13), jnp.float32)
    parent = parent.at[1:, 0].set(branch.astype(jnp.float32))
    parent = parent.at[1:, 1:].set(leaf_link.astype(jnp.float32))
    ancestor = (
        jnp.eye(13, dtype=jnp.float32) + parent + jnp.dot(parent, parent, precision=PRECISE_MATMUL)
    )
    depth_table = jnp.concatenate(
        [jnp.zeros((1,), jnp.int32), jnp.where(branch, 1, 2).astype(jnp.int32)]
    )
    labels = jnp.arange(13, dtype=jnp.int32)
    member = segment[:, None] == labels[None, :]
    depth_rank = jnp.sum(jnp.where(member, depth_table[None, :], 0), axis=1)
    positions = (
        offset + jnp.where(depth_rank >= 1, TRUNK, 0) + jnp.where(depth_rank == 2, BRANCH, 0)
    )
    return (member.astype(jnp.float32), ancestor, positions)


def path_mask(member, ancestor, positions):
    reached_slots = jnp.dot(
        jnp.dot(member, ancestor, precision=PRECISE_MATMUL), member.T, precision=PRECISE_MATMUL
    )
    return (reached_slots > 0.5) & (positions[None, :] <= positions[:, None])


def rope_tables(positions):
    frequency = BASE_FREQ ** (-jnp.arange(0, HEAD_DIM, 2, dtype=jnp.float32) / HEAD_DIM)
    angles = positions.astype(jnp.float32)[:, None] * frequency[None, :]
    cos_half = jnp.cos(angles)
    sin_half = jnp.sin(angles)
    return (
        jnp.concatenate([cos_half, cos_half], axis=-1),
        jnp.concatenate([sin_half, sin_half], axis=-1),
    )


def rotate(tensor, cos_table, sin_table):
    half_dim = tensor.shape[-1] // 2
    turned = jnp.concatenate([-tensor[..., half_dim:], tensor[..., :half_dim]], axis=-1)
    return tensor * cos_table[:, None, :] + turned * sin_table[:, None, :]


def unrotate(tensor, cos_table, sin_table):
    half_dim = tensor.shape[-1] // 2
    shifted = tensor * sin_table[:, None, :]
    return tensor * cos_table[:, None, :] + jnp.concatenate(
        [shifted[..., half_dim:], -shifted[..., :half_dim]], axis=-1
    )


def scores_of(query_tree, key_tree, member, ancestor, positions):
    allowed = path_mask(member, ancestor, positions)
    raw = jnp.einsum(
        "qhd,khd->hqk", query_tree, key_tree, preferred_element_type=jnp.float32
    ) * HEAD_DIM ** (-0.5)
    return jnp.where(allowed[None], raw, MASKED_SCORE)


def attend(tree_block):
    query_tree, key_tree, value_tree, member, ancestor, positions = tree_block
    scores = scores_of(query_tree, key_tree, member, ancestor, positions)
    top_score = jnp.max(scores, axis=2, keepdims=True)
    weights = jnp.exp(scores - top_score)
    total = jnp.sum(weights, axis=2, keepdims=True)
    attn_probs = weights / total
    context = jnp.einsum(
        "hqk,khd->qhd",
        attn_probs.astype(jnp.bfloat16),
        value_tree,
        preferred_element_type=jnp.float32,
    )
    return (context.astype(jnp.bfloat16), top_score[..., 0] + jnp.log(total[..., 0]))


def attend_back(tree_block):
    query_tree, key_tree, value_tree, context_grad, log_total, member, ancestor, positions = (
        tree_block
    )
    scores = scores_of(query_tree, key_tree, member, ancestor, positions)
    attn_probs = jnp.exp(scores - log_total[..., None])
    prob_grad = jnp.einsum(
        "qhd,khd->hqk", context_grad, value_tree, preferred_element_type=jnp.float32
    )
    score_grad = attn_probs * (prob_grad - jnp.sum(attn_probs * prob_grad, axis=2, keepdims=True))
    score_low = score_grad.astype(jnp.bfloat16)
    scale = HEAD_DIM ** (-0.5)
    query_grad = (
        jnp.einsum("hqk,khd->qhd", score_low, key_tree, preferred_element_type=jnp.float32) * scale
    )
    key_grad = (
        jnp.einsum("hqk,qhd->khd", score_low, query_tree, preferred_element_type=jnp.float32)
        * scale
    )
    value_grad = jnp.einsum(
        "hqk,qhd->khd",
        attn_probs.astype(jnp.bfloat16),
        context_grad,
        preferred_element_type=jnp.float32,
    )
    return (query_grad, key_grad, value_grad)


MESH_ID = pl.DeviceIdType.MESH


def flip(index, step):
    if step == 0:
        return index
    if step == 1:
        return index + 1 - 2 * lax.rem(index, 2)
    if step == 2:
        return lax.rem(index + 2, 4)
    return 3 - index


def places(lo_count, tp_count):
    hi, lo, tp = lax.axis_index("hi"), lax.axis_index("lo"), lax.axis_index("tp")

    def along(step):
        return {"hi": flip(hi, step), "lo": lo, "tp": tp}

    def across(q):
        return {"hi": hi, "lo": q // tp_count, "tp": lax.rem(q, tp_count)}

    return hi, lo * tp_count + tp, along, across


def greet(plane, me, along, across):
    barrier = pltpu.get_barrier_semaphore()
    for step in range(1, 4):
        pl.semaphore_signal(barrier, inc=1, device_id=along(step), device_id_type=MESH_ID)

    def one(q, carry):
        @pl.when(q != me)
        def _():
            pl.semaphore_signal(barrier, inc=1, device_id=across(q), device_id_type=MESH_ID)

        return carry

    lax.fori_loop(0, plane, one, 0)
    pl.semaphore_wait(barrier, 3 + plane - 1)


def wait_bytes(ref, sem):
    pltpu.make_async_copy(ref, ref, sem).wait()


def spread_kernel(
    lo_count,
    tp_count,
    cap_pad,
    half_count,
    rows_ref,
    pick_ref,
    router_ref,
    gate_up_ref,
    arrived_ref,
    pre_ref,
    gate_ref,
    far_ref,
    send_ref,
    chunk_ref,
    weight_ref,
    out_ref,
    far_send,
    far_recv,
    near_send,
    near_recv,
    own_sem,
    load_sem,
    weight_sem,
    out_sem,
):
    plane = lo_count * tp_count
    hi, me, along, across = places(lo_count, tp_count)
    count = plane * cap_pad
    width = rows_ref.shape[1]
    wide = gate_up_ref.shape[2]
    fill = pltpu.make_async_copy(gate_up_ref, weight_ref, weight_sem)
    fill.start()
    greet(plane, me, along, across)

    def far_copy(step):
        return pltpu.make_async_remote_copy(
            src_ref=rows_ref,
            dst_ref=far_ref.at[step - 1],
            send_sem=far_send.at[step - 1],
            recv_sem=far_recv.at[step - 1],
            device_id=along(step),
            device_id_type=MESH_ID,
        )

    def near_copy(step, slot, q):
        return pltpu.make_async_remote_copy(
            src_ref=send_ref.at[slot, pl.ds(pl.multiple_of(q * cap_pad, 16), cap_pad)],
            dst_ref=arrived_ref.at[step, pl.ds(pl.multiple_of(me * cap_pad, 16), cap_pad)],
            send_sem=near_send.at[step],
            recv_sem=near_recv.at[step],
            device_id=across(q),
            device_id_type=MESH_ID,
        )

    def own_copy(step, slot):
        return pltpu.make_async_copy(
            send_ref.at[slot, pl.ds(pl.multiple_of(me * cap_pad, 16), cap_pad)],
            arrived_ref.at[step, pl.ds(pl.multiple_of(me * cap_pad, 16), cap_pad)],
            own_sem.at[step],
        )

    others = pl.ds(0, count - cap_pad)

    def sent(step):
        wait_bytes(send_ref.at[step % 2, others], near_send.at[step])

    def select(step):
        slot = step % 2
        if step >= 2:
            sent(step - 2)

        def one(turn, carry):
            q = lax.rem(me + 1 + turn, plane)
            start = pl.multiple_of(q * cap_pad, 16)
            rows = rows_ref[...] if step == 0 else far_ref[step - 1]
            picked = jnp.dot(
                pick_ref[step, pl.ds(start, cap_pad)], rows, preferred_element_type=jnp.float32
            )
            send_ref[slot, pl.ds(start, cap_pad)] = picked.astype(jnp.bfloat16)

            @pl.when(q != me)
            def _():
                near_copy(step, slot, q).start()

            @pl.when(q == me)
            def _():
                own_copy(step, slot).start()

            return carry

        lax.fori_loop(0, plane, one, 0)

    def out_copy(step):
        return pltpu.make_async_copy(out_ref.at[step % 2], pre_ref.at[step], out_sem.at[step % 2])

    def forward(step):
        wait_bytes(arrived_ref.at[step, others], near_recv.at[step])
        own_copy(step, step % 2).wait()
        load = pltpu.make_async_copy(arrived_ref.at[step], chunk_ref, load_sem)
        load.start()
        load.wait()
        logits = jnp.dot(chunk_ref[...], router_ref[...], preferred_element_type=jnp.float32)
        weights = jnp.exp(logits - jnp.max(logits, axis=1, keepdims=True))
        own_expert = (hi * plane + me) * half_count // 2
        lanes = lax.broadcasted_iota(jnp.int32, weights.shape, 1)
        own = jnp.sum(jnp.where(lanes == own_expert, weights, 0.0), axis=1, keepdims=True)
        gate_ref[step] = own / jnp.sum(weights, axis=1, keepdims=True)
        if step == 0:
            fill.wait()
        if step >= 2:
            out_copy(step - 2).wait()
        tile = 256

        def one(index, carry):
            half = index // (wide // tile)
            start = pl.multiple_of(lax.rem(index, wide // tile) * tile, tile)
            out = jnp.dot(
                chunk_ref[...],
                weight_ref[half, :, pl.ds(start, tile)],
                preferred_element_type=jnp.float32,
            )
            out_ref[step % 2, :, pl.ds(pl.multiple_of(index * tile, tile), tile)] = out.astype(
                jnp.bfloat16
            )
            return carry

        lax.fori_loop(0, half_count * (wide // tile), one, 0)
        out_copy(step).start()

    far_copy(1).start()
    far_copy(2).start()
    select(0)
    far_copy(1).wait_recv()
    select(1)
    forward(0)
    far_copy(2).wait_recv()
    far_copy(3).start()
    select(2)
    forward(1)
    far_copy(3).wait_recv()
    select(3)
    forward(2)
    forward(3)
    for step in (2, 3):
        sent(step)
        out_copy(step).wait()
    for step in (1, 2, 3):
        far_copy(step).wait_send()


def spread(lo_count, tp_count, cap_pad, half_count, rows, pick, router, gate_up):
    plane = lo_count * tp_count
    count = plane * cap_pad
    width = rows.shape[1]
    wide = half_count * gate_up.shape[2]
    whole = pl.BlockSpec(memory_space=pltpu.VMEM)
    anywhere = pl.BlockSpec(memory_space=pl.ANY)
    return pl.pallas_call(
        functools.partial(spread_kernel, lo_count, tp_count, cap_pad, half_count),
        out_shape=(
            jax.ShapeDtypeStruct((4, count, width), jnp.bfloat16),
            jax.ShapeDtypeStruct((4, count, wide), jnp.bfloat16),
            jax.ShapeDtypeStruct((4, count, 1), jnp.float32),
        ),
        in_specs=[whole, whole, whole, anywhere],
        out_specs=(anywhere, anywhere, whole),
        scratch_shapes=[
            pltpu.VMEM((3,) + rows.shape, jnp.bfloat16),
            pltpu.VMEM((2, count, width), jnp.bfloat16),
            pltpu.VMEM((count, width), jnp.bfloat16),
            pltpu.VMEM(gate_up.shape, jnp.bfloat16),
            pltpu.VMEM((2, count, wide), jnp.bfloat16),
            pltpu.SemaphoreType.DMA((3,)),
            pltpu.SemaphoreType.DMA((3,)),
            pltpu.SemaphoreType.DMA((4,)),
            pltpu.SemaphoreType.DMA((4,)),
            pltpu.SemaphoreType.DMA((4,)),
            pltpu.SemaphoreType.DMA,
            pltpu.SemaphoreType.DMA,
            pltpu.SemaphoreType.DMA((2,)),
        ],
        compiler_params=pltpu.CompilerParams(
            collective_id=1, has_side_effects=True, vmem_limit_bytes=VMEM_BYTES
        ),
        cost_estimate=pl.CostEstimate(
            flops=8 * count * width * (wide + rows.shape[0]),
            bytes_accessed=16 * count * width,
            transcendentals=0,
        ),
    )(rows, pick, router, gate_up)


def gather_kernel(
    lo_count,
    tp_count,
    cap_pad,
    half_count,
    pre_ref,
    cot_0,
    cot_1,
    cot_2,
    cot_3,
    gate_ref,
    gate_up_hbm,
    down_hbm,
    back_ref,
    arrived_ref,
    grad_ref,
    gate_up_grad,
    down_grad,
    share_ref,
    low_ref,
    land_ref,
    land_out,
    home_ref,
    pre_buf,
    cot_buf,
    weight_ref,
    down_ref,
    hidden_ref,
    send_ref,
    tile_buf,
    part_ref,
    home_buf,
    sum_buf,
    share_buf,
    left_buf,
    out_buf,
    wide_buf,
    dot_ref,
    weight_sem,
    load_sem,
    store_sem,
    near_send,
    near_recv,
    own_sem,
    out_send,
    out_recv,
    out_own,
    share_sem,
    tile_sem,
    home_sem,
    sum_sem,
    far_send,
    far_recv,
    left_sem,
    right_sem,
    out_sem,
):
    plane = lo_count * tp_count
    hi, me, along, across = places(lo_count, tp_count)
    count = plane * cap_pad
    cot_refs = (cot_0, cot_1, cot_2, cot_3)
    width = cot_0.shape[1]
    wide = pre_ref.shape[2]
    half_wide = wide // half_count
    ff_half = half_wide // 2
    units = half_count * ff_half
    payload = width + 128
    rows = back_ref.shape[1]
    own_expert = (hi * plane + me) * half_count // 2
    tile = 256
    order = (3, 2, 1, 0)
    fill_down = pltpu.make_async_copy(down_hbm, down_ref, weight_sem.at[0])
    fill_gate_up = pltpu.make_async_copy(
        gate_up_hbm, weight_ref.at[pl.ds(0, half_count * width)], weight_sem.at[1]
    )

    def load_pre(step):
        return pltpu.make_async_copy(pre_ref.at[step], pre_buf, load_sem.at[0])

    def load_cot(step):
        return pltpu.make_async_copy(cot_refs[step], cot_buf, load_sem.at[1])

    def store(step):
        return pltpu.make_async_copy(pre_buf, low_ref.at[step], store_sem.at[0])

    fill_down.start()
    load_pre(order[0]).start()
    load_cot(order[0]).start()
    fill_gate_up.start()
    greet(plane, me, along, across)

    def block(q):
        return pl.ds(pl.multiple_of(q * cap_pad, 16), cap_pad)

    others = pl.ds(0, count - cap_pad)

    def near_copy(step, q):
        return pltpu.make_async_remote_copy(
            src_ref=send_ref.at[step, block(q)],
            dst_ref=land_ref.at[step, block(me)],
            send_sem=near_send.at[step],
            recv_sem=near_recv.at[step],
            device_id=across(q),
            device_id_type=MESH_ID,
        )

    def own_copy(step):
        return pltpu.make_async_copy(
            send_ref.at[step, block(me)], land_ref.at[step, block(me)], own_sem.at[step]
        )

    def out_near(step, q):
        return pltpu.make_async_remote_copy(
            src_ref=send_ref.at[step, block(q), pl.ds(0, width)],
            dst_ref=land_out.at[step, block(me)],
            send_sem=out_send.at[step],
            recv_sem=out_recv.at[step],
            device_id=across(q),
            device_id_type=MESH_ID,
        )

    def out_self(step):
        return pltpu.make_async_copy(
            send_ref.at[step, block(me), pl.ds(0, width)],
            land_out.at[step, block(me)],
            out_own.at[step],
        )

    def far_copy(step):
        return pltpu.make_async_remote_copy(
            src_ref=part_ref.at[step % 2],
            dst_ref=home_ref.at[step - 1],
            send_sem=far_send.at[step - 1],
            recv_sem=far_recv.at[step - 1],
            device_id=along(step),
            device_id_type=MESH_ID,
        )

    def backward(turn):
        step = order[turn]
        if turn == 0:
            fill_down.wait()
        load_pre(step).wait()
        load_cot(step).wait()
        dot_ref[...] = jnp.zeros(dot_ref.shape, jnp.float32)

        def act(index, carry):
            half = index // (ff_half // tile)
            inner = lax.rem(index, ff_half // tile) * tile
            gate_at = pl.ds(pl.multiple_of(half * half_wide + inner, tile), tile)
            up_at = pl.ds(pl.multiple_of(half * half_wide + ff_half + inner, tile), tile)
            unit_at = pl.ds(pl.multiple_of(index * tile, tile), tile)
            raw = lax.dot_general(
                cot_buf[...],
                down_ref[unit_at, :],
                (((1,), (1,)), ((), ())),
                preferred_element_type=jnp.float32,
            )
            gate_pre = pre_buf[:, gate_at].astype(jnp.float32)
            up_pre = pre_buf[:, up_at].astype(jnp.float32)
            gate = gate_ref[step]
            sigmoid = 1.0 / (1.0 + jnp.exp(-gate_pre))
            swish = gate_pre * sigmoid
            hidden = swish * up_pre
            dot_ref[...] += jnp.sum(raw * hidden, axis=1, keepdims=True)
            hidden_ref[step * count : (step + 1) * count, unit_at] = (hidden * gate).astype(
                jnp.bfloat16
            )
            act_grad = raw * gate
            pre_buf[:, gate_at] = (
                act_grad * up_pre * (sigmoid + swish * (1.0 - sigmoid))
            ).astype(jnp.bfloat16)
            pre_buf[:, up_at] = (act_grad * swish).astype(jnp.bfloat16)
            return carry

        lax.fori_loop(0, half_count * (ff_half // tile), act, 0)
        store(step).start()
        if turn < 3:
            load_cot(order[turn + 1]).start()
        if turn == 0:
            fill_gate_up.wait()
        def down(index, carry):
            start = pl.multiple_of(index * tile, tile)
            total = None
            for half in range(half_count):
                part = lax.dot_general(
                    pre_buf[:, half * half_wide : (half + 1) * half_wide],
                    weight_ref[pl.ds(half * width + start, tile), pl.ds(0, half_wide)],
                    (((1,), (1,)), ((), ())),
                    preferred_element_type=jnp.float32,
                )
                total = part if total is None else total + part
            send_ref[step, :, pl.ds(start, tile)] = total.astype(jnp.bfloat16)
            return carry

        lax.fori_loop(0, width // tile, down, 0)
        lanes = lax.broadcasted_iota(jnp.int32, (count, 128), 1)
        send_ref[step, :, width:payload] = jnp.where(
            lanes == own_expert, dot_ref[...], 0.0
        ).astype(jnp.bfloat16)

        send(lambda q: near_copy(step, q), lambda: own_copy(step))
        store(step).wait()
        if turn < 3:
            load_pre(order[turn + 1]).start()

    def send(remote_copy, local_copy):
        def one(turn, carry):
            q = lax.rem(me + 1 + turn, plane)

            @pl.when(q != me)
            def _():
                remote_copy(q).start()

            @pl.when(q == me)
            def _():
                local_copy().start()

            return carry

        lax.fori_loop(0, plane, one, 0)

    def outward(step):
        wait_bytes(send_ref.at[step, others], near_send.at[step])
        if step == 0:
            own_copy(step).wait()

        def one(index, carry):
            at = pl.ds(pl.multiple_of(index * tile, tile), tile)
            out = jnp.dot(
                hidden_ref[step * count : (step + 1) * count, :],
                down_ref[:, at],
                preferred_element_type=jnp.float32,
            )
            send_ref[step, :, at] = out.astype(jnp.bfloat16)
            return carry

        lax.fori_loop(0, width // tile, one, 0)
        send(lambda q: out_near(step, q), lambda: out_self(step))

    lumps = [(start, min(256, payload - start)) for start in range(0, payload, 256)]

    def tile_copy(step, lump):
        start, size = lumps[lump]
        return pltpu.make_async_copy(
            land_ref.at[step, :, pl.ds(start, size)],
            tile_buf.at[lump % 2, :, pl.ds(0, size)],
            tile_sem.at[lump % 2],
        )

    def home_copy(lump):
        start, size = lumps[lump]
        return pltpu.make_async_copy(
            home_ref.at[:, :, pl.ds(start, size)],
            home_buf.at[lump % 2, :, :, pl.ds(0, size)],
            home_sem.at[lump % 2],
        )

    def sum_copy(lump):
        start, size = lumps[lump]
        return pltpu.make_async_copy(
            sum_buf.at[lump % 2, :, pl.ds(0, size)],
            grad_ref.at[:, pl.ds(start, size)],
            sum_sem.at[lump % 2],
        )

    def merge(step):
        wait_bytes(land_ref.at[step, others], near_recv.at[step])
        if step > 0:
            own_copy(step).wait()
        if step == 1:
            far_copy(3).wait_send()
        if step == 0:
            for far in (1, 2, 3):
                far_copy(far).wait_recv()
            home_copy(0).start()
        tile_copy(step, 0).start()
        for lump, (start, size) in enumerate(lumps):
            if lump + 1 < len(lumps):
                tile_copy(step, lump + 1).start()
                if step == 0:
                    home_copy(lump + 1).start()
            tile_copy(step, lump).wait()
            total = jnp.dot(
                back_ref[step],
                tile_buf[lump % 2, :, :size],
                preferred_element_type=jnp.float32,
            )
            if step == 0:
                home_copy(lump).wait()
                for far in range(3):
                    total = total + home_buf[lump % 2, far, :, :size].astype(jnp.float32)
                if lump >= 2:
                    sum_copy(lump - 2).wait()
                sum_buf[lump % 2, :, :size] = total
                sum_copy(lump).start()
            else:
                part_ref[step % 2, :, start : start + size] = total.astype(jnp.bfloat16)
        if step == 0:
            sum_copy(len(lumps) - 2).wait()
            sum_copy(len(lumps) - 1).wait()
        else:
            far_copy(step).start()

    def share_copy(step, lump):
        start, size = lumps[lump]
        return pltpu.make_async_copy(
            share_buf.at[lump % 2, :, pl.ds(0, size)],
            share_ref.at[flip(hi, step), :, pl.ds(start, size)],
            share_sem.at[lump % 2],
        )

    def out_tile(step, lump):
        start, size = lumps[lump]
        return pltpu.make_async_copy(
            land_out.at[step, :, pl.ds(start, size)],
            tile_buf.at[lump % 2, :, pl.ds(0, size)],
            tile_sem.at[lump % 2],
        )

    def merge_out(step):
        wait_bytes(land_out.at[step, others], out_recv.at[step])
        out_self(step).wait()
        out_tile(step, 0).start()
        out_lumps = width // 256
        for lump in range(out_lumps):
            if lump + 1 < out_lumps:
                out_tile(step, lump + 1).start()
            out_tile(step, lump).wait()
            total = jnp.dot(
                back_ref[step], tile_buf[lump % 2], preferred_element_type=jnp.float32
            )
            if lump >= 2:
                share_copy(step, lump - 2).wait()
            share_buf[lump % 2] = total.astype(jnp.bfloat16)
            share_copy(step, lump).start()
        share_copy(step, out_lumps - 2).wait()
        share_copy(step, out_lumps - 1).wait()

    slots = 4 * count

    def right_copies(source, start):
        return [
            pltpu.make_async_copy(
                ref.at[:, pl.ds(start, half_wide)],
                weight_ref.at[pl.ds(index * count, count), pl.ds(0, half_wide)],
                right_sem.at[index],
            )
            for index, ref in enumerate(source)
        ]

    def left_copies(source, index, slot):
        at = pl.ds(pl.multiple_of(index * tile, tile), tile)
        return [
            pltpu.make_async_copy(
                source.at[step, :, at],
                left_buf.at[slot, pl.ds(step * count, count)],
                left_sem.at[slot, step],
            )
            for step in range(4)
        ]

    def product(left):
        return lax.dot_general(
            left,
            weight_ref[pl.ds(0, slots), pl.ds(0, half_wide)],
            (((0,), (0,)), ((), ())),
            preferred_element_type=jnp.float32,
        )

    def weight_grad(left, right, right_start, tiles, write, out_copy, depth):
        copies = right_copies(right, right_start)
        for copy in copies:
            copy.start()
        if left is not None:
            for copy in left_copies(left, 0, 0):
                copy.start()
        for copy in copies:
            copy.wait()

        def one(index, carry):
            slot = lax.rem(index, 2)

            if left is None:
                result = product(hidden_ref[:, pl.ds(pl.multiple_of(index * tile, tile), tile)])
            else:

                @pl.when(index + 1 < tiles)
                def _():
                    for copy in left_copies(left, index + 1, 1 - slot):
                        copy.start()

                for copy in left_copies(left, index, slot):
                    copy.wait()
                result = product(left_buf[slot])

            @pl.when(index >= depth)
            def _():
                out_copy(index - depth, lax.rem(index, depth)).wait()

            write(lax.rem(index, depth), result)
            out_copy(index, lax.rem(index, depth)).start()
            return carry

        lax.fori_loop(0, tiles, one, 0)
        for index in range(max(tiles - depth, 0), tiles):
            out_copy(index, index % depth).wait()

    def gate_up_part(half):
        groups = half_wide // 128
        per = ff_half // 128

        def write(slot, result):
            for group in range(groups):
                row = (group % per) * 2 + group // per
                out_buf[slot, pl.ds(row, tile, stride=groups), :] = result[
                    :, group * 128 : (group + 1) * 128
                ]

        def out_copy(index, slot):
            return pltpu.make_async_copy(
                out_buf.at[slot],
                gate_up_grad.at[
                    pl.ds(pl.multiple_of((half * width + index * tile) * groups, 8), tile * groups)
                ],
                out_sem.at[slot],
            )

        low_parts = [low_ref.at[step] for step in range(4)]
        weight_grad(arrived_ref, low_parts, half * half_wide, width // tile, write, out_copy, 2)

    def down_part(part):
        def write(slot, result):
            wide_buf[...] = result

        def out_copy(index, slot):
            return pltpu.make_async_copy(
                wide_buf,
                down_grad.at[
                    pl.ds(pl.multiple_of(index * tile, tile), tile),
                    pl.ds(part * half_wide, half_wide),
                ],
                out_sem.at[slot],
            )

        weight_grad(None, cot_refs, part * half_wide, units // tile, write, out_copy, 1)

    for turn in range(4):
        backward(turn)
    merge(3)
    outward(3)
    merge(2)
    outward(2)
    gate_up_part(0)
    merge(1)
    outward(1)
    outward(0)
    merge(0)
    for half in range(1, half_count):
        gate_up_part(half)
    merge_out(3)
    for part in range(width // half_wide):
        down_part(part)
    for step in (2, 1, 0):
        merge_out(step)
    for step in range(4):
        wait_bytes(send_ref.at[step, others, pl.ds(0, width)], out_send.at[step])
    for step in (1, 2):
        far_copy(step).wait_send()


def gather(
    lo_count, tp_count, cap_pad, half_count, pre, cots, gate, gate_up, down, back, arrived
):
    plane = lo_count * tp_count
    count = plane * cap_pad
    width = cots[0].shape[1]
    wide = pre.shape[2]
    half_wide = wide // half_count
    units = down.shape[0]
    rows = back.shape[1]
    payload = width + 128
    whole = pl.BlockSpec(memory_space=pltpu.VMEM)
    anywhere = pl.BlockSpec(memory_space=pl.ANY)
    sem = pltpu.SemaphoreType.DMA
    low = jnp.bfloat16
    outs = pl.pallas_call(
        functools.partial(gather_kernel, lo_count, tp_count, cap_pad, half_count),
        out_shape=(
            jax.ShapeDtypeStruct((rows, payload), jnp.float32),
            jax.ShapeDtypeStruct((width * wide // 128, 128), jnp.float32),
            jax.ShapeDtypeStruct((units, width), jnp.float32),
            jax.ShapeDtypeStruct((4, rows, width), low),
            jax.ShapeDtypeStruct((4, count, wide), low),
            jax.ShapeDtypeStruct((4, count, payload), low),
            jax.ShapeDtypeStruct((4, count, width), low),
            jax.ShapeDtypeStruct((3, rows, payload), low),
        ),
        in_specs=[anywhere] * 5 + [whole, anywhere, anywhere, whole, anywhere],
        out_specs=(anywhere,) * 8,
        scratch_shapes=[
            pltpu.VMEM((count, wide), low),
            pltpu.VMEM((count, width), low),
            pltpu.VMEM((max(half_count * width, 4 * count), half_wide), low),
            pltpu.VMEM(down.shape, low),
            pltpu.VMEM((4 * count, units), low),
            pltpu.VMEM((4, count, payload), low),
            pltpu.VMEM((2, count, 256), low),
            pltpu.VMEM((2, rows, payload), low),
            pltpu.VMEM((2, 3, rows, 256), low),
            pltpu.VMEM((2, rows, 256), jnp.float32),
            pltpu.VMEM((2, rows, 256), low),
            pltpu.VMEM((2, 4 * count, 256), low),
            pltpu.VMEM((2, 256 * half_wide // 128, 128), jnp.float32),
            pltpu.VMEM((256, half_wide), jnp.float32),
            pltpu.VMEM((count, 1), jnp.float32),
            sem((2,)),
            sem((2,)),
            sem((2,)),
            sem((4,)),
            sem((4,)),
            sem((4,)),
            sem((4,)),
            sem((4,)),
            sem((4,)),
            sem((2,)),
            sem((2,)),
            sem((2,)),
            sem((2,)),
            sem((3,)),
            sem((3,)),
            sem((2, 4)),
            sem((4,)),
            sem((2,)),
        ],
        compiler_params=pltpu.CompilerParams(
            collective_id=2, has_side_effects=True, vmem_limit_bytes=VMEM_BYTES
        ),
        cost_estimate=pl.CostEstimate(
            flops=48 * count * width * units,
            bytes_accessed=40 * count * width,
            transcendentals=0,
        ),
    )(pre, *cots, gate, gate_up, down, back, arrived)
    return outs[:4]


def tail_kernel(
    lo_count,
    y_count,
    pieces,
    query_part,
    key_part,
    value_part,
    rows_part,
    hidden_ref,
    mixed_ref,
    gain_ref,
    qk_ref,
    sum_ref,
    input_ref,
    gain_sum_ref,
    near_lo,
    half_ref,
    near_hi,
    full_ref,
    stage_ref,
    keep_ref,
    twin_ref,
    near_y,
    own_ref,
    gain_send,
    gain_recv,
    lo_send,
    lo_recv,
    hi_send,
    hi_recv,
    hi_back_send,
    hi_back_recv,
    lo_back_send,
    lo_back_recv,
    row_sem,
    y_send,
    y_recv,
    y_back_send,
    y_back_recv,
    stage_sem,
    gain_send_sem,
    gain_recv_sem,
):
    parts = (query_part, key_part, value_part)
    hi, lo, tp = lax.axis_index("hi"), lax.axis_index("lo"), lax.axis_index("tp")
    core = lax.rem(tp, 2)
    y = tp // 2
    block_rows = full_ref.shape[4]

    def at_hi(step):
        return {"hi": flip(hi, step), "lo": lo, "tp": tp}

    def at_lo(step):
        return {"hi": hi, "lo": lax.rem(lo + step, lo_count), "tp": tp}

    def at_y(step):
        return {"hi": hi, "lo": lo, "tp": lax.rem(y + step, y_count) * 2 + core}

    twin = {"hi": hi, "lo": lo, "tp": tp + 1 - 2 * core}

    def remote(src, dst, send_sem, recv_sem, device):
        return pltpu.make_async_remote_copy(
            src_ref=src,
            dst_ref=dst,
            send_sem=send_sem,
            recv_sem=recv_sem,
            device_id=device,
            device_id_type=MESH_ID,
        )

    los, his, ys = range(1, lo_count), range(1, 4), range(1, y_count)
    barrier = pltpu.get_barrier_semaphore()
    peers = [twin] + [at_y(s) for s in ys] + [at_lo(s) for s in los] + [at_hi(s) for s in his]
    for peer in peers:
        pl.semaphore_signal(barrier, inc=1, device_id=peer, device_id_type=MESH_ID)
    pl.semaphore_wait(barrier, len(peers))

    to_twin = remote(
        rows_part.at[:, 1 - core], twin_ref, row_sem.at[0], row_sem.at[1], twin
    )
    to_twin.start()
    keep_load = pltpu.make_async_copy(rows_part.at[:, core], keep_ref, row_sem.at[2])
    keep_load.start()

    def lo_copy(step, piece, part):
        return remote(
            parts[part].at[lax.rem(lo + step, lo_count), :, piece],
            near_lo.at[step - 1, piece, part],
            lo_send.at[step - 1, piece, part],
            lo_recv.at[step - 1, piece, part],
            at_lo(step),
        )

    def hi_copy(step, piece):
        return remote(
            half_ref.at[piece, :, flip(hi, step)],
            near_hi.at[step - 1, piece],
            hi_send.at[step - 1, piece],
            hi_recv.at[step - 1, piece],
            at_hi(step),
        )

    def hi_back(step, piece):
        return remote(
            full_ref.at[:, lo, hi, piece],
            full_ref.at[:, lo, hi, piece],
            hi_back_send.at[step - 1, piece],
            hi_back_recv.at[step - 1, piece],
            at_hi(step),
        )

    def lo_back(step, piece):
        return remote(
            full_ref.at[:, lo, :, piece],
            full_ref.at[:, lo, :, piece],
            lo_back_send.at[step - 1, piece],
            lo_back_recv.at[step - 1, piece],
            at_lo(step),
        )

    def y_copy(step):
        return remote(
            keep_ref.at[lax.rem(y + step, y_count)],
            near_y.at[step - 1],
            y_send.at[step - 1],
            y_recv.at[step - 1],
            at_y(step),
        )

    def y_back(step):
        return remote(
            own_ref,
            input_ref.at[y, core],
            y_back_send.at[step - 1],
            y_back_recv.at[step - 1],
            at_y(step),
        )

    def twin_back():
        return remote(
            input_ref.at[:, core], input_ref.at[:, core], row_sem.at[3], row_sem.at[4], twin
        )

    for piece in range(pieces):
        for part in range(3):
            for step in los:
                lo_copy(step, piece, part).start()

    keep_load.wait()
    to_twin.wait()
    rows = own_ref.shape[0]
    row_tile = 32

    def add_twin(index, carry):
        place, start = index // (rows // row_tile), lax.rem(index, rows // row_tile) * row_tile
        at = pl.ds(pl.multiple_of(start, row_tile), row_tile)
        keep_ref[place, at, :] = (
            keep_ref[place, at, :].astype(jnp.float32) + twin_ref[place, at, :].astype(jnp.float32)
        ).astype(jnp.bfloat16)
        return carry

    lax.fori_loop(0, y_count * (rows // row_tile), add_twin, 0)
    for step in ys:
        y_copy(step).start()

    def add_lo(piece):
        for part in range(3):
            for step in los:
                lo_copy(step, piece, part).wait_recv()
            for place in range(4):
                total = parts[part][lo, place, piece].astype(jnp.float32)
                for step in los:
                    total = total + near_lo[step - 1, piece, part, place].astype(jnp.float32)
                half_ref[piece, part, place] = total.astype(jnp.bfloat16)
        for step in his:
            hi_copy(step, piece).start()

    def add_hi(piece):
        for step in his:
            hi_copy(step, piece).wait_recv()
        for part in range(3):
            total = half_ref[piece, part, hi].astype(jnp.float32)
            for step in his:
                total = total + near_hi[step - 1, piece, part].astype(jnp.float32)
            full_ref[part, lo, hi, piece] = total.astype(jnp.bfloat16)
        for step in his:
            hi_back(step, piece).start()

    def spread_lo(piece):
        for step in his:
            hi_back(step, piece).wait_recv()
        for step in los:
            lo_back(step, piece).start()

    def gain_copy(stage, slot, device):
        return remote(
            gain_send.at[stage],
            gain_recv.at[slot],
            gain_send_sem.at[slot],
            gain_recv_sem.at[slot],
            device,
        )

    gain_stages = [[twin], [at_y(s) for s in ys], [at_lo(s) for s in los], [at_hi(s) for s in his]]
    gain_slots = []
    slot = 0
    for stage in gain_stages:
        gain_slots.append(list(range(slot, slot + len(stage))))
        slot += len(stage)

    def gain_start(stage):
        for slot, device in zip(gain_slots[stage], gain_stages[stage]):
            gain_copy(stage, slot, device).start()

    def gain_finish(stage):
        total = gain_send[stage]
        for slot, device in zip(gain_slots[stage], gain_stages[stage]):
            gain_copy(stage, slot, device).wait_recv()
            total = total + gain_recv[slot]
        if stage == 1:
            gain_send[2, 0:8] = total[0:8]
            gain_send[2, 8:16] = qk_ref[...]
        elif stage + 1 < len(gain_stages):
            gain_send[stage + 1] = total
        else:
            gain_sum_ref[...] = total

    add_lo(0)
    for step in ys:
        y_copy(step).wait_recv()
    gain_send[0] = jnp.zeros(gain_send.shape[1:], jnp.float32)

    def back(index, carry):
        at = pl.ds(pl.multiple_of(index * row_tile, row_tile), row_tile)
        grad = keep_ref[y, at, :].astype(jnp.float32)
        for step in ys:
            grad = grad + near_y[step - 1, at, :].astype(jnp.float32)
        value = hidden_ref[at, :].astype(jnp.float32)
        inverse = lax.rsqrt(jnp.mean(value * value, axis=1, keepdims=True) + EPSILON)
        unit = value * inverse
        scaled = grad * gain_ref[...]
        product = grad * unit
        gain_send[0, 0:8] += jnp.sum(product.reshape(row_tile // 8, 8, product.shape[1]), axis=0)
        mean = jnp.mean(scaled * unit, axis=1, keepdims=True)
        own_ref[at, :] = (mixed_ref[at, :] + inverse * (scaled - unit * mean)).astype(jnp.bfloat16)
        return carry

    lax.fori_loop(0, rows // row_tile, back, 0)
    own_store = pltpu.make_async_copy(own_ref, input_ref.at[y, core], row_sem.at[2])
    own_store.start()
    for step in ys:
        y_back(step).start()
    gain_start(0)
    for piece in range(1, pieces):
        add_lo(piece)
    gain_finish(0)
    gain_start(1)
    add_hi(0)
    gain_finish(1)
    gain_start(2)
    add_hi(1)
    gain_finish(2)
    gain_start(3)
    spread_lo(0)
    gain_finish(3)
    own_store.wait()
    for step in ys:
        y_back(step).wait_recv()
    twin_back().start()
    for piece in range(2, pieces):
        add_hi(piece)
        spread_lo(piece - 1)
    spread_lo(pieces - 1)

    def stage_copy(turn, part, piece, place):
        return pltpu.make_async_copy(
            stage_ref.at[turn], sum_ref.at[part, place, :, piece], stage_sem.at[turn]
        )

    turn = 0
    for group in range(lo_count):
        for piece in range(pieces):
            place = lax.rem(lo + lo_count - group, lo_count)
            if group > 0:
                lo_back(group, piece).wait_recv()
            for part in range(3):
                if turn >= 2:
                    stage_copy(turn % 2, part, piece, place).wait()
                stage_ref[turn % 2] = full_ref[part, place, :, piece].astype(jnp.float32)
                stage_copy(turn % 2, part, piece, place).start()
                turn += 1
    stage_copy(0, 0, 0, lo).wait()
    stage_copy(1, 0, 0, lo).wait()
    twin_back().wait()
    for step in ys:
        y_copy(step).wait_send()
        y_back(step).wait_send()
    for piece in range(pieces):
        for step in los:
            for part in range(3):
                lo_copy(step, piece, part).wait_send()
            lo_back(step, piece).wait_send()
        for step in his:
            hi_copy(step, piece).wait_send()
            hi_back(step, piece).wait_send()
    for stage, slots in enumerate(gain_slots):
        for slot, device in zip(slots, gain_stages[stage]):
            gain_copy(stage, slot, device).wait_send()


def tail(lo_count, tp_count, parts, rows_part, hidden_own, mixed_grad, gain, qk_rows):
    y_count = tp_count // 2
    depth, wide = parts[0].shape
    rows, width = hidden_own.shape
    pieces = 4
    block = depth // (lo_count * 4 * pieces)
    cut = (lo_count, 4, pieces, block, wide)
    parts = [part.reshape(cut) for part in parts]
    rows_part = rows_part.reshape(y_count, 2, rows, width)
    whole = pl.BlockSpec(memory_space=pltpu.VMEM)
    anywhere = pl.BlockSpec(memory_space=pl.ANY)
    gain_slots = 1 + (y_count - 1) + (lo_count - 1) + 3
    sem = pltpu.SemaphoreType.DMA
    lo_n, y_n = lo_count - 1, y_count - 1
    sums, input_grad, gain_sum = pl.pallas_call(
        functools.partial(tail_kernel, lo_count, y_count, pieces),
        out_shape=(
            jax.ShapeDtypeStruct((3,) + cut, jnp.float32),
            jax.ShapeDtypeStruct((y_count, 2, rows, width), jnp.bfloat16),
            jax.ShapeDtypeStruct((16, width), jnp.float32),
        ),
        in_specs=[whole] * 3 + [anywhere] + [whole] * 4,
        out_specs=(anywhere, anywhere, whole),
        scratch_shapes=[
            pltpu.VMEM((lo_n, pieces, 3, 4, block, wide), jnp.bfloat16),
            pltpu.VMEM((pieces, 3, 4, block, wide), jnp.bfloat16),
            pltpu.VMEM((3, pieces, 3, block, wide), jnp.bfloat16),
            pltpu.VMEM((3,) + cut, jnp.bfloat16),
            pltpu.VMEM((2, 4, block, wide), jnp.float32),
            pltpu.VMEM((y_count, rows, width), jnp.bfloat16),
            pltpu.VMEM((y_count, rows, width), jnp.bfloat16),
            pltpu.VMEM((y_n, rows, width), jnp.bfloat16),
            pltpu.VMEM((rows, width), jnp.bfloat16),
            pltpu.VMEM((4, 16, width), jnp.float32),
            pltpu.VMEM((gain_slots, 16, width), jnp.float32),
            sem((lo_n, pieces, 3)),
            sem((lo_n, pieces, 3)),
            sem((3, pieces)),
            sem((3, pieces)),
            sem((3, pieces)),
            sem((3, pieces)),
            sem((lo_n, pieces)),
            sem((lo_n, pieces)),
            sem((5,)),
            sem((y_n,)),
            sem((y_n,)),
            sem((y_n,)),
            sem((y_n,)),
            sem((2,)),
            sem((gain_slots,)),
            sem((gain_slots,)),
        ],
        compiler_params=pltpu.CompilerParams(
            collective_id=3, has_side_effects=True, vmem_limit_bytes=VMEM_BYTES
        ),
        cost_estimate=pl.CostEstimate(
            flops=16 * rows * width, bytes_accessed=16 * depth * wide, transcendentals=0
        ),
    )(*parts, rows_part, hidden_own, mixed_grad, gain, qk_rows)
    return (
        sums.reshape(3, depth, wide).transpose(1, 0, 2),
        input_grad.reshape(y_count * 2 * rows, width),
        jnp.sum(gain_sum[:8], axis=0),
        gain_sum[8:10, :wide],
    )


def shards(
    hidden,
    cotangent,
    norm_gains,
    qkv_weight,
    qk_gain,
    out_weight,
    router_weight,
    gate_up,
    down_weight,
    routes,
    parents,
):
    tp_count = lax.axis_size("tp")
    hi_count = lax.axis_size("hi")
    lo_count = lax.axis_size("lo")
    tp_rank = lax.axis_index("tp")
    hi_rank = lax.axis_index("hi")
    exp = ("hi", "lo")
    world = ("hi", "lo", "tp")
    plane = lo_count * tp_count
    device_count = hi_count * plane
    rows_all, model_width = hidden.shape
    rows_own = cotangent.shape[0]
    local_width = qkv_weight.shape[2]
    local_heads = local_width // HEAD_DIM
    expert_count = router_weight.shape[1]
    half_count = gate_up.shape[0]
    ff_half = gate_up.shape[3]
    top_count = routes.shape[1]
    capacity = (9 * rows_own * top_count + 8 * expert_count - 1) // (8 * expert_count)
    cap_pad = -(-capacity // 16) * 16
    tree_count = parents.shape[0]
    tree_len = rows_all // tree_count
    own_start = tp_rank * rows_own

    own_routes = lax.dynamic_slice_in_dim(routes, own_start, rows_own, 0)
    labels = jnp.arange(expert_count, dtype=jnp.int32)
    hits = jnp.any(own_routes[:, :, None] == labels[None, None, :], axis=1)
    row_ids = jnp.arange(rows_own, dtype=jnp.int32)
    earlier = (row_ids[:, None] > row_ids[None, :]).astype(jnp.bfloat16)
    slots = jnp.dot(earlier, hits.astype(jnp.bfloat16), preferred_element_type=jnp.float32).astype(
        jnp.int32
    )
    kept = hits & (slots < capacity)
    codes = jnp.where(kept, slots, -1)
    copies = device_count // expert_count
    near_count = plane // copies

    def along(block, step):
        return lax.ppermute(block, "hi", [(i, i ^ step) for i in range(hi_count)])

    tie = lax.optimization_barrier
    codes_turned = codes.T.astype(jnp.bfloat16)
    codes_all = jnp.stack(
        [codes_turned] + [along(codes_turned, step) for step in range(1, hi_count)]
    )
    near_codes = lax.dynamic_slice_in_dim(codes_all, hi_rank * near_count, near_count, 1)
    near_codes = near_codes.astype(jnp.int32)
    if copies > 1:
        near_codes = jnp.repeat(near_codes, copies, axis=1)
    slot_ids = jnp.arange(cap_pad, dtype=jnp.int32)
    pick = (
        (near_codes[:, :, None, :] == slot_ids[None, None, :, None])
        .astype(jnp.bfloat16)
        .reshape(hi_count, plane * cap_pad, rows_own)
    )
    back = pick.transpose(0, 2, 1)

    def across(block):
        moved = lax.all_to_all(
            block.reshape(plane, cap_pad, model_width),
            ("lo", "tp"),
            split_axis=0,
            concat_axis=0,
            tiled=True,
        )
        return moved.reshape(plane * cap_pad, model_width)

    cot_all = lax.all_gather(cotangent, "hi", axis=0, tiled=False)

    def pick_cot(step):
        rows = cotangent
        if step > 0:
            rows = lax.dynamic_index_in_dim(cot_all, hi_rank ^ step, 0, keepdims=False)
        picked = jnp.dot(pick[step], rows, preferred_element_type=jnp.float32)
        return across(picked.astype(jnp.bfloat16))

    cot_arrived = [pick_cot(0)]
    hidden, pick = tie((hidden, pick))

    member, ancestor, positions = jax.vmap(tree_layout)(parents)
    cos_table, sin_table = rope_tables(positions.reshape(-1))
    hidden_f = hidden.astype(jnp.float32)
    unit_one, inverse_one = normalize(hidden_f)
    normed_one = (unit_one * norm_gains[0]).astype(jnp.bfloat16)
    qkv_flat = qkv_weight.reshape(model_width, 3 * local_width)
    qkv_all = jnp.dot(normed_one, qkv_flat, preferred_element_type=jnp.float32)
    query_raw = qkv_all[:, :local_width]
    key_raw = qkv_all[:, local_width : 2 * local_width]
    value_raw = qkv_all[:, 2 * local_width :]
    query_sq, key_sq = lax.psum(
        (jnp.sum(query_raw * query_raw, axis=1), jnp.sum(key_raw * key_raw, axis=1)), "tp"
    )
    query_inv = lax.rsqrt(query_sq / model_width + EPSILON)[:, None]
    key_inv = lax.rsqrt(key_sq / model_width + EPSILON)[:, None]
    query_hat = query_raw * query_inv
    key_hat = key_raw * key_inv
    head_shape = (rows_all, local_heads, HEAD_DIM)
    query_low = rotate((query_hat * qk_gain[0]).reshape(head_shape), cos_table, sin_table).astype(
        jnp.bfloat16
    )
    key_low = rotate((key_hat * qk_gain[1]).reshape(head_shape), cos_table, sin_table).astype(
        jnp.bfloat16
    )
    value_low = value_raw.reshape(head_shape).astype(jnp.bfloat16)
    tree_shape = (tree_count, tree_len, local_heads, HEAD_DIM)
    query_trees = query_low.reshape(tree_shape)
    key_trees = key_low.reshape(tree_shape)
    value_trees = value_low.reshape(tree_shape)
    query_trees, arrived_first = tie((query_trees, cot_arrived[0]))
    cot_arrived = [arrived_first, pick_cot(1)]
    context_low, log_total = lax.map(
        attend, (query_trees, key_trees, value_trees, member, ancestor, positions)
    )
    context_low = context_low.reshape(rows_all, local_width)
    context_low, arrived_second = tie((context_low, cot_arrived[1]))
    cot_arrived = [arrived_first, arrived_second, pick_cot(2), pick_cot(3)]
    attention = lax.psum_scatter(
        jnp.dot(context_low, out_weight, preferred_element_type=jnp.float32).astype(jnp.bfloat16),
        "tp",
        scatter_dimension=0,
        tiled=True,
    ).astype(jnp.float32)
    hidden_own = lax.dynamic_slice_in_dim(hidden, own_start, rows_own, 0).astype(jnp.float32)
    mixed = hidden_own + attention
    unit_two, inverse_two = normalize(mixed)
    normed_two = (unit_two * norm_gains[1]).astype(jnp.bfloat16)
    logits = jnp.dot(normed_two, router_weight, preferred_element_type=jnp.float32)
    route_probs = softmax_rows(logits)

    gate_up_flat = gate_up.reshape(half_count, model_width, 2 * ff_half)
    down_flat = down_weight.reshape(half_count * ff_half, model_width)
    sizes = (lo_count, tp_count, cap_pad, half_count)
    arrived, pre_act, gate = spread(*sizes, normed_two, pick, router_weight, gate_up_flat)
    returned, gate_up_grad, down_grad, share = gather(
        *sizes,
        pre_act,
        cot_arrived,
        gate,
        gate_up_flat.reshape(half_count * model_width, 2 * ff_half),
        down_flat,
        back,
        arrived,
    )
    expert_grad = returned[:, :model_width]
    prob_grad = returned[:, model_width : model_width + expert_count]
    gate_up_grad = gate_up_grad.reshape(half_count, model_width, ff_half // 128, 2, 128)
    gate_up_grad = gate_up_grad.transpose(0, 1, 3, 2, 4).reshape(gate_up.shape)
    down_grad = down_grad.reshape(down_weight.shape)

    logit_grad = route_probs * (prob_grad - jnp.sum(route_probs * prob_grad, axis=1, keepdims=True))
    logit_low = logit_grad.astype(jnp.bfloat16)
    normed_grad = expert_grad + jnp.dot(
        logit_low, router_weight.T, preferred_element_type=jnp.float32
    )
    router_part = lax.dot_general(
        logit_low, normed_two, (((0,), (0,)), ((), ())), preferred_element_type=jnp.float32
    )
    gain_two_grad = jnp.sum(normed_grad * unit_two, axis=0)
    mixed_grad = cotangent.astype(jnp.float32) + norm_back(
        normed_grad, unit_two, inverse_two, norm_gains[1]
    )
    small_rows = -(-(expert_count + 1) // 16) * 16
    parts = [mixed_grad, router_part, gain_two_grad[None]]
    parts.append(jnp.zeros((small_rows - expert_count - 1, model_width), jnp.float32))
    gathered = lax.all_gather(
        jnp.concatenate([part.astype(jnp.bfloat16) for part in parts]), "tp", axis=0, tiled=False
    )
    share, gathered = tie((share, gathered))
    mixed_low = gathered[:, :rows_own].reshape(rows_all, model_width)
    small = jnp.sum(gathered[:, rows_own:].astype(jnp.float32), axis=0)
    out_weight_grad = jnp.dot(context_low.T, mixed_low, preferred_element_type=jnp.float32)
    context_grad = jnp.dot(mixed_low, out_weight.T, preferred_element_type=jnp.float32).astype(
        jnp.bfloat16
    )
    out_low = jnp.concatenate([out_weight_grad.astype(jnp.bfloat16), small.astype(jnp.bfloat16)])
    out_low, context_grad = tie((out_low, context_grad))
    out_sum = lax.psum(out_low, exp)
    share, out_sum = tie((share, out_sum))
    expert_sum = lax.psum_scatter(
        share.reshape(hi_count * rows_own, model_width), "hi", scatter_dimension=0, tiled=True
    )
    query_grad, key_grad, value_grad = lax.map(
        attend_back,
        (
            query_trees,
            key_trees,
            value_trees,
            context_grad.reshape(tree_shape),
            log_total,
            member,
            ancestor,
            positions,
        ),
    )
    query_grad, share = tie((query_grad, share))
    query_grad = unrotate(query_grad.reshape(head_shape), cos_table, sin_table).reshape(
        rows_all, local_width
    )
    key_grad = unrotate(key_grad.reshape(head_shape), cos_table, sin_table).reshape(
        rows_all, local_width
    )
    query_gain_grad = jnp.sum(query_grad * query_hat, axis=0)
    key_gain_grad = jnp.sum(key_grad * key_hat, axis=0)
    qk_rows = jnp.pad(
        jnp.stack([query_gain_grad, key_gain_grad]), ((0, 6), (0, model_width - local_width))
    )
    query_hat_grad = query_grad * qk_gain[0]
    key_hat_grad = key_grad * qk_gain[1]
    query_dot, key_dot = lax.psum(
        (jnp.sum(query_hat_grad * query_hat, axis=1), jnp.sum(key_hat_grad * key_hat, axis=1)), "tp"
    )
    query_raw_grad = query_inv * (query_hat_grad - query_hat * (query_dot / model_width)[:, None])
    key_raw_grad = key_inv * (key_hat_grad - key_hat * (key_dot / model_width)[:, None])
    qkv_grad_low = jnp.concatenate(
        [query_raw_grad, key_raw_grad, value_grad.reshape(rows_all, local_width)], axis=1
    ).astype(jnp.bfloat16)
    normed_part = jnp.dot(
        qkv_grad_low, qkv_flat.T, preferred_element_type=jnp.float32
    ).astype(jnp.bfloat16)
    weight_parts = [
        lax.dot_general(
            normed_one,
            qkv_grad_low[:, part * local_width : (part + 1) * local_width],
            (((0,), (0,)), ((), ())),
            preferred_element_type=jnp.float32,
        ).astype(jnp.bfloat16)
        for part in range(3)
    ]
    qkv_sum, input_grad, gain_one, qk_sum = tail(
        lo_count,
        tp_count,
        weight_parts,
        normed_part,
        lax.dynamic_slice_in_dim(hidden, own_start, rows_own, 0),
        mixed_grad,
        norm_gains[:1],
        qk_rows,
    )
    layer_out = (mixed + expert_sum.astype(jnp.float32)).astype(jnp.bfloat16)
    out_sum = out_sum.astype(jnp.float32)
    small = out_sum[local_width:]
    return (
        layer_out,
        input_grad,
        jnp.stack([gain_one, small[expert_count]]),
        qkv_sum,
        qk_sum,
        out_sum[:local_width],
        small[:expert_count].T,
        gate_up_grad,
        down_grad,
    )


def solution(mesh):
    exp_count, tp_count = mesh.devices.shape
    split = jax.sharding.Mesh(
        mesh.devices.reshape(4, exp_count // 4, tp_count), ("hi", "lo", "tp")
    )
    exp = ("hi", "lo")
    return jax.shard_map(
        shards,
        mesh=split,
        in_specs=(
            P(exp, None),
            P(("hi", "lo", "tp"), None),
            P(),
            P(None, None, "tp"),
            P(None, "tp"),
            P("tp", None),
            P(),
            P(("hi", "lo", "tp"), None, None, None),
            P(("hi", "lo", "tp"), None, None),
            P(exp, None),
            P(exp, None),
        ),
        out_specs=(
            P(("hi", "lo", "tp"), None),
            P(exp, None),
            P(),
            P(None, None, "tp"),
            P(None, "tp"),
            P("tp", None),
            P(),
            P(("hi", "lo", "tp"), None, None, None),
            P(("hi", "lo", "tp"), None, None),
        ),
        check_vma=False,
    )
```
